512 devices in a mesh: sub: 16 (over y_lo, x, core), tile: 32 (over z, y_hi).
Axes of the slice: x: 4, y: 8 (y_hi: 4, y_lo: 2; y = y_hi * 2 + y_lo), z: 8, core: 2. Of those that a mesh axis runs over, the one named last changes fastest.
Arguments:
- states: float32 [16, 3, 1024, 2048], P('sub', None, 'tile'), may hold values from -6 to 6
- terrain: int32 [1024, 2048], P('tile'), may hold values from 0 to 7
- depth_table: float32 [8], replicated, may hold values from 0.5 to 2
- spread_table: float32 [8], replicated, may hold values from 0.03 to 0.24
- mixing: float32 [16, 16], replicated, may hold values from -0.9 to 2, as said below
Outputs:
- gradient: float32 [16, 3, 1024, 2048], P('sub', None, 'tile')
The draws below stay inside these ranges and needn't reach their ends.
Inputs may be any that keep to these rules, and one draw needn't show every extreme that they name: `mixing`: A dense matrix with diagonal entries between 1 and 2.
All inputs are finite; a program needn't handle non-finite values.
Results may differ from the reference program's by a relative error of at most 0.00012.
Values sent between devices are 32-bit elements; how exact they have to be, the bound alone decides.
No kernel may reach another device: no remote copies, remote signals or barrier semaphores. Data moves between devices by JAX's collectives and lax.ppermute only.
A program may use at most 64 MiB of HBM per device.

```python
import math
import jax
import jax.numpy as jnp
from jax import lax

NY = 2048
NCLASS = 8
FSTEPS = 3
DSTEPS = 3
S = 16
NX = 1024


def draw_mixing(key, part):
    first_key = jax.random.fold_in(key, 11)
    second_key = jax.random.fold_in(key, 12)
    diagonal = jax.random.uniform(first_key, (S,), jnp.float32, 1.0, 2.0)
    off = jnp.clip(0.3 * jax.random.normal(second_key, (S, S), jnp.float32), -0.9, 0.9)
    eye = jnp.eye(S, dtype=jnp.float32)
    return off * (1.0 - eye) + eye * diagonal[None, :]


def touch_ends(entries, stream_key, smallest, largest):
    longest = entries.shape.index(max(entries.shape))
    spots = []
    for shift in (0, 1):
        where = [jax.random.randint(jax.random.fold_in(stream_key, axis), (), 0, length) for axis, length in enumerate(entries.shape)]
        where[longest] = (where[longest] + shift) % entries.shape[longest]
        spots.append(tuple(where))
    return entries.at[spots[0]].set(smallest).at[spots[1]].set(largest)


def steps_of(rng, extent, cuts, smallest, largest):
    def one(position, blocks):
        heights = jax.random.uniform(jax.random.fold_in(jax.random.fold_in(rng, 6), position), (blocks,), jnp.float32, smallest / len(cuts), largest / len(cuts))
        return jnp.repeat(jnp.exp(heights), extent[position] // blocks).reshape((-1,) + (1,) * (len(extent) - position - 1))

    gain = one(*cuts[0])
    for cut in cuts[1:]:
        gain = gain * one(*cut)
    return gain


def scatter_about(rng, shape, width, bound, shards=(), kind=jnp.bfloat16):
    entries = jax.random.normal(rng, shape, jnp.float32) * width
    if len(shards) > 0:
        entries = steps_of(rng, shape, shards, -0.22, 0.18) * entries
    return jnp.clip(entries, min=-bound, max=bound).astype(kind)


def setup_inputs(seed: int = 0) -> dict:
    keys = jax.random.split(jax.random.key(seed), 6)
    return {
        "states": scatter_about(keys[0], (S, 3, NX, NY), 1.0, 6.0, ((0, 16), (2, 32)), jnp.float32),
        "terrain": touch_ends(jax.random.randint(keys[1], (NX, NY), 0, NCLASS), jax.random.fold_in(keys[1], 1), 0, NCLASS - 1).astype(jnp.int32),
        "depth_table": jnp.clip(jnp.exp(jax.random.uniform(keys[2], (NCLASS,), jnp.float32, math.log(0.5), math.log(2.0))), 0.5, 2.0),
        "spread_table": jnp.clip(jax.random.uniform(keys[3], (NCLASS,), jnp.float32, 0.03, 0.24), 0.03, 0.24),
        "mixing": draw_mixing(jax.random.fold_in(keys[5], 71), 0),
    }


time_step = 0.5
gravity = 1.0
coriolis = 0.3


def col_diff(field):
    return (jnp.roll(field, -1, -1) - jnp.roll(field, 1, -1)) * 0.5


def row_mask(first, count, total):
    index = first + jnp.arange(count, dtype=jnp.int32)
    return ((index >= 0) & (index < total)).astype(jnp.float32)[:, None]


def model_step(state, depth, first, total):
    height, east, north = state[0], state[1], state[2]
    flux_x = depth * east
    flux_y = depth * north
    new_h = height[1:-1] - time_step * ((flux_x[2:] - flux_x[:-2]) * 0.5 + col_diff(flux_y[1:-1]))
    new_h = new_h * row_mask(first + 1, new_h.shape[0], total)
    new_u = east[2:-2] - time_step * gravity * (new_h[2:] - new_h[:-2]) * 0.5 + time_step * coriolis * north[2:-2]
    new_v = north[2:-2] - time_step * gravity * col_diff(new_h[1:-1]) - time_step * coriolis * east[2:-2]
    result = jnp.stack([new_h[1:-1], new_u, new_v])
    return result * row_mask(first + 2, result.shape[1], total)


def spread_step(field, kappa, first, total):
    centre = field[:, 1:-1]
    laplace = field[:, 2:] + field[:, :-2] + jnp.roll(centre, 1, 2) + jnp.roll(centre, -1, 2) - 4.0 * centre
    return (centre + kappa * laplace) * row_mask(first + 1, centre.shape[1], total)


def reference(states, terrain, depth_table, spread_table, mixing):
    classes = jnp.arange(NCLASS, dtype=jnp.int32)
    pick = (terrain[None] == classes[:, None, None]).astype(jnp.float32)
    depth = jnp.sum(pick * depth_table[:, None, None], 0)
    kappa = jnp.sum(pick * spread_table[:, None, None], 0)
    depth_pad = jnp.pad(depth, ((2, 2), (0, 0)))

    def forward(state):
        for step in range(FSTEPS):
            padded = jnp.pad(state, ((0, 0), (2, 2), (0, 0)))
            state = model_step(padded, depth_pad, -2, NX)
        return state

    ends = lax.map(forward, states)
    earlier = jnp.concatenate([jnp.zeros_like(ends[:1]), ends[:-1]], 0)
    jumps = states - earlier
    mixed = jnp.einsum("st,tfxy->sfxy", mixing, jumps, precision=lax.Precision.HIGHEST)

    def smooth(field):
        for step in range(DSTEPS):
            padded = jnp.pad(field, ((0, 0), (1, 1), (0, 0)))
            field = spread_step(padded, kappa, -1, NX)
        return field

    return lax.map(smooth, mixed)
```

```python
import jax
import jax.numpy as jnp
from jax import lax
from jax.experimental import pallas as pl
from jax.experimental.pallas import tpu as pltpu
from jax.sharding import PartitionSpec as P

FSTEPS = 3
DSTEPS = 3
S = 16
F = 3
G = 4
L = 128
R = 9
W = 2 * R
NMAIN = F * G

VMEM = pl.BlockSpec(memory_space=pltpu.VMEM)
SMEM = pl.BlockSpec(memory_space=pltpu.SMEM)
F32 = jnp.float32


def iota(dim, shape=(8, L)):
    return lax.broadcasted_iota(jnp.int32, shape, dim)


def lookup(classes, table):
    value = jnp.full(classes.shape, table[0], F32)
    for i in range(1, table.shape[0]):
        value = jnp.where(classes == i, table[i], value)
    return value


def pack_kernel(x_ref, o_ref):
    lane = iota(1)

    def tile(f, g, c):
        return x_ref[f, 8 * g : 8 * g + 8, L * (c % S) : L * (c % S) + L]

    for c in range(S):
        for f in range(F):
            for g in range(G):
                o_ref[c, f * G + g] = tile(f, g, c)
        for j in range(2):
            packed = jnp.zeros((8, L), F32)
            for q in range(6):
                f, g = q % 3, 2 * j + q // 3
                sides = jnp.where(lane < 64, tile(f, g, c + 1), tile(f, g, c - 1))
                sides = pltpu.roll(sides, W * q + R, 1)
                packed = jnp.where((lane >= W * q) & (lane < W * q + W), sides, packed)
            o_ref[c, NMAIN + j] = packed


def terrain_tiles(ter_ref, chunk, g):
    def tile(c):
        start = pl.multiple_of(lax.rem(c + S, S) * L, L)
        return ter_ref[8 * g : 8 * g + 8, pl.ds(start, L)]

    return tile(chunk), jnp.where(iota(1) < 64, tile(chunk + 1), tile(chunk - 1))


def edge_kernel(chunk_ref, depth_ref, x_ref, ter_ref, up_ref, down_ref):
    lane, row = iota(1), iota(0)
    chunk = chunk_ref[0]

    def depth_of(g, q):
        own, sides = terrain_tiles(ter_ref, chunk, g)
        return lookup(own, depth_ref), pltpu.roll(lookup(sides, depth_ref), W * q + R, 1)

    def send(o_ref, g, inner, edge, turn, sign, halo, flux_at, height_at, even_by, odd_by):
        depth_own, depth_sides = depth_of(inner, flux_at)
        own, sides = terrain_tiles(ter_ref, chunk, g)
        o_ref[56] = own.astype(F32)
        sides = pltpu.roll(sides.astype(F32), 108 + R, 1)
        at_edge = row == edge
        at_height = at_edge & (lane >= W * height_at) & (lane < W * height_at + W)
        by = (W * (height_at - flux_at)) % L
        packed = []
        for t in range(S):
            flux = pltpu.roll(depth_own * x_ref[t, G + inner], turn, 0)
            o_ref[t * F] = x_ref[t, g] + jnp.where(at_edge, sign * flux, 0.0)
            o_ref[t * F + 1] = x_ref[t, G + g]
            o_ref[t * F + 2] = x_ref[t, 2 * G + g]
            columns = x_ref[t, NMAIN + halo]
            flux = pltpu.roll(pltpu.roll(depth_sides * columns, by, 1), turn, 0)
            columns = columns + jnp.where(at_height, sign * flux, 0.0)
            shift = odd_by if t % 2 else even_by
            packed.append(pltpu.roll(columns, shift, 1) if shift else columns)
        for j in range(S // 2):
            o_ref[48 + j] = jnp.where(
                lane < 54, packed[2 * j], jnp.where(lane < 108, packed[2 * j + 1], sides)
            )

    send(up_ref, 0, 1, 7, 7, -0.25, 0, 4, 0, 0, 54)
    send(down_ref, 3, 2, 0, 1, 0.25, 1, 1, 3, L - 54, 0)


def main_kernel(
    place_ref, depth_ref, spread_ref, mix_ref, x_ref, ter_ref, above_ref, below_ref,
    o_ref, depth_s, kappa_s, ends_s, jumps_s,
):
    rows, cols = 8 * (G + 2), 2 * L
    chunk, first, total = place_ref[0], place_ref[1], place_ref[2]
    row = iota(0, (rows, cols))
    index = row + (first - 8)
    inside = ((index >= 0) & (index < total)).astype(F32)
    slope = -0.25 * inside

    def back(value, by):
        return pltpu.roll(value, (L - by) % L, 1)

    def grid(tiles):
        return jnp.concatenate([jnp.concatenate(pair, axis=1) for pair in tiles], axis=0)

    def terrain_halo(ref):
        return ref[56].astype(jnp.int32), back(ref[48], 108 + R).astype(jnp.int32)

    classes = grid(
        [terrain_halo(above_ref)]
        + [terrain_tiles(ter_ref, chunk, g) for g in range(G)]
        + [terrain_halo(below_ref)]
    )
    depth_s[...] = lookup(classes, depth_ref)
    kappa_s[...] = lookup(classes, spread_ref) * inside
    ends_s[...] = jnp.zeros(ends_s.shape, F32)

    def before(value, dim):
        return pltpu.roll(value, 1, dim)

    def after(value, dim):
        return pltpu.roll(value, value.shape[dim] - 1, dim)

    def model(h, u, v, outer):
        depth = depth_s[...]
        flux_x, flux_y = depth * u, depth * v
        up, down = before(flux_x, 0), after(flux_x, 0)
        if outer:
            up = jnp.where(row == 0, 0.0, up)
            down = jnp.where(row == rows - 1, 0.0, down)
        h = h + slope * ((down - up) + (after(flux_y, 1) - before(flux_y, 1)))
        new_u = u + slope * (after(h, 0) - before(h, 0)) + 0.15 * v
        new_v = v - 0.25 * (after(h, 1) - before(h, 1)) - 0.15 * u
        return h, new_u, new_v

    def spread(w):
        kappa = kappa_s[...]
        around = (after(w, 0) + before(w, 0)) + (after(w, 1) + before(w, 1))
        return (1.0 - 4.0 * kappa) * w + kappa * around

    def one(t, half, pair):
        state = []
        for f in range(F):
            by = W * f + 54 * half + R
            tiles = [(above_ref[t * F + f], back(above_ref[48 + pair], by))]
            for g in range(G):
                q = (g % 2) * 3 + f
                tiles.append((x_ref[t, f * G + g], back(x_ref[t, NMAIN + g // 2], W * q + R)))
            tiles.append((below_ref[t * F + f], back(below_ref[48 + pair], by)))
            state.append(grid(tiles))
        jumps = [state[f] - ends_s[f] for f in range(F)]
        for step in range(FSTEPS):
            state = model(*state, step == 0)
        for f in range(F):
            ends_s[f] = state[f]
        for f in range(F):
            w = jumps[f]
            for step in range(DSTEPS):
                w = spread(w)
            for g in range(G):
                jumps_s[t, f * G + g] = w[8 + 8 * g : 16 + 8 * g, :L]

    def two(pair, carry):
        one(2 * pair, 0, pair)
        one(2 * pair + 1, 1, pair)
        return carry

    lax.fori_loop(0, S // 2, two, 0)

    def mix(part, carry):
        base = part * 3
        held = [[jumps_s[t, base + i] for i in range(3)] for t in range(S)]
        for s in range(S):
            sums = [mix_ref[s, 0] * held[0][i] for i in range(3)]
            for t in range(1, S):
                weight = mix_ref[s, t]
                sums = [sums[i] + weight * held[t][i] for i in range(3)]
            for i in range(3):
                o_ref[s, base + i] = sums[i]
        return carry

    lax.fori_loop(0, NMAIN // 3, mix, 0)


def local(states, terrain, depth_table, spread_table, mixing):
    strips = lax.axis_size("tile")
    rows = states.shape[2]
    chunk = lax.axis_index("sub").astype(jnp.int32)
    first = lax.axis_index("tile").astype(jnp.int32) * rows
    place = jnp.stack([chunk, first, jnp.int32(rows * strips)])

    chunks = pl.pallas_call(
        pack_kernel,
        out_shape=jax.ShapeDtypeStruct((S, NMAIN + 2, 8, L), F32),
        in_specs=[VMEM],
        out_specs=VMEM,
    )(states[0])
    held = lax.all_to_all(chunks, "sub", split_axis=0, concat_axis=0, tiled=True)
    halo = jax.ShapeDtypeStruct((57, 8, L), F32)
    up, down = pl.pallas_call(
        edge_kernel,
        out_shape=(halo, halo),
        in_specs=[SMEM, SMEM, VMEM, VMEM],
        out_specs=(VMEM, VMEM),
    )(place, depth_table, held, terrain)
    forth = [(i, i + 1) for i in range(strips - 1)]
    above = lax.ppermute(down, "tile", forth)
    below = lax.ppermute(up, "tile", [(j, i) for i, j in forth])
    wide = (8 * (G + 2), 2 * L)
    mixed = pl.pallas_call(
        main_kernel,
        out_shape=jax.ShapeDtypeStruct((S, NMAIN, 8, L), F32),
        in_specs=[SMEM, SMEM, SMEM, SMEM, VMEM, VMEM, VMEM, VMEM],
        out_specs=VMEM,
        scratch_shapes=[
            pltpu.VMEM(wide, F32),
            pltpu.VMEM(wide, F32),
            pltpu.VMEM((F,) + wide, F32),
            pltpu.VMEM((S, NMAIN, 8, L), F32),
        ],
    )(place, depth_table, spread_table, mixing, held, terrain, above, below)
    parts = lax.all_to_all(mixed, "sub", split_axis=0, concat_axis=0, tiled=True)
    parts = parts.reshape(S, F, rows, L).transpose(1, 2, 0, 3)
    return parts.reshape(1, F, rows, S * L)


def solution(mesh):
    in_specs = (P("sub", None, "tile", None), P("tile", None), P(), P(), P())
    out_specs = P("sub", None, "tile", None)
    return jax.shard_map(local, mesh=mesh, in_specs=in_specs, out_specs=out_specs, check_vma=False)
```

```python
import jax
import jax.numpy as jnp
from jax import lax
from jax.experimental import pallas as pl
from jax.experimental.pallas import tpu as pltpu
from jax.sharding import PartitionSpec as P

FSTEPS = 3
DSTEPS = 3
S = 16
F = 3
G = 4
L = 128
R = 8
C = 9
W = 2 * C
NMAIN = F * G
NALL = NMAIN + 2
NHALO = S * F + S // 2
BLOCKS = 8
DEPTH = 6
EDGE = 16
TALL = L + 2 * EDGE
PART = 16

VMEM = pl.BlockSpec(memory_space=pltpu.VMEM)
SMEM = pl.BlockSpec(memory_space=pltpu.SMEM)
F32 = jnp.float32


def iota(dim, shape=(8, L)):
    return lax.broadcasted_iota(jnp.int32, shape, dim)


def lookup(classes, table):
    value = jnp.full(classes.shape, table[0], F32)
    for i in range(1, table.shape[0]):
        value = jnp.where(classes == i, table[i], value)
    return value


def pack_kernel(x_ref, o_ref):
    lane = iota(1)

    def tile(f, g, c):
        return x_ref[f, 8 * g : 8 * g + 8, L * (c % S) : L * (c % S) + L]

    for c in range(S):
        for f in range(F):
            for g in range(G):
                o_ref[c, f * G + g] = tile(f, g, c)
        for j in range(2):
            packed = jnp.zeros((8, L), F32)
            for q in range(6):
                f, g = q % 3, 2 * j + q // 3
                sides = jnp.where(lane < 64, tile(f, g, c + 1), tile(f, g, c - 1))
                sides = pltpu.roll(sides, W * q + C, 1)
                packed = jnp.where((lane >= W * q) & (lane < W * q + W), sides, packed)
            o_ref[c, NMAIN + j] = packed


def terrain_tiles(ter_ref, chunk, g):
    def tile(c):
        start = pl.multiple_of(lax.rem(c + S, S) * L, L)
        return ter_ref[8 * g : 8 * g + 8, pl.ds(start, L)]

    return tile(chunk), jnp.where(iota(1) < 64, tile(chunk + 1), tile(chunk - 1))


def edge_kernel(place_ref, depth_ref, x_ref, ter_ref, up_ref, down_ref):
    lane, row = iota(1), iota(0)
    chunk = place_ref[0]

    def send(o_ref, g, inner, edge, turn, sign, halo, flux_at, height_at, low_by, high_by):
        own, sides = terrain_tiles(ter_ref, chunk, inner)
        depth_own = sign * lookup(own, depth_ref)
        depth_sides = pltpu.roll(sign * lookup(sides, depth_ref), W * flux_at + C, 1)
        at_edge = row == edge
        at_height = at_edge & (lane >= W * height_at) & (lane < W * height_at + W)
        by = (W * (height_at - flux_at)) % L
        packed = []
        for t in range(S):
            flux = pltpu.roll(depth_own * x_ref[t, G + inner], turn, 0)
            o_ref[t * F] = x_ref[t, g] + jnp.where(at_edge, flux, 0.0)
            o_ref[t * F + 1] = x_ref[t, G + g]
            o_ref[t * F + 2] = x_ref[t, 2 * G + g]
            columns = x_ref[t, NMAIN + halo]
            flux = pltpu.roll(pltpu.roll(depth_sides * columns, by, 1), turn, 0)
            columns = columns + jnp.where(at_height, flux, 0.0)
            shift = low_by if t < S // 2 else high_by
            packed.append(pltpu.roll(columns, shift, 1) if shift else columns)
        for j in range(S // 2):
            o_ref[S * F + j] = jnp.where(lane < 3 * W, packed[j], packed[j + S // 2])

    send(up_ref, 0, 1, 7, 7, -0.25, 0, 4, 0, 0, 3 * W)
    send(down_ref, 3, 2, 0, 1, 0.25, 1, 1, 3, L - 3 * W, 0)


def terrain_kernel(place_ref, ter_ref, up_ref, down_ref):
    up_ref[0], up_ref[1] = terrain_tiles(ter_ref, place_ref[0], 0)
    down_ref[0], down_ref[1] = terrain_tiles(ter_ref, place_ref[0], G - 1)


def row_of(block, r):
    return DEPTH * block + r - R


def inside_of(first, total, r, shape):
    index = DEPTH * lax.div(iota(1, shape), S) + (r - R) + first
    return ((index >= 0) & (index < total)).astype(F32)


def coef_kernel(place_ref, depth_ref, spread_ref, ter_ref, above_ref, below_ref, o_ref, table_s):
    chunk, first, total = place_ref[0], place_ref[1], place_ref[2]
    lane = iota(1)
    tiles = [(above_ref[0], above_ref[1])]
    tiles += [terrain_tiles(ter_ref, chunk, g) for g in range(G)]
    tiles += [(below_ref[0], below_ref[1])]
    for i, (own, sides) in enumerate(tiles):
        rows = slice(8 * i, 8 * i + 8)
        table_s[0, rows] = lookup(own, depth_ref)
        table_s[1, rows] = lookup(own, spread_ref)
        depth = pltpu.roll(lookup(sides, depth_ref), C, 1)
        spread = pltpu.roll(lookup(sides, spread_ref), W + C, 1)
        table_s[2, rows] = jnp.where(lane < W, depth, spread)
    for r in range(DEPTH):
        inside = inside_of(first, total, r, (1, L))

        def turned(k):
            rows = [
                jnp.broadcast_to(table_s[k, pl.ds(row_of(b, r) + R, 1), :], (S, L))
                for b in range(BLOCKS)
            ]
            return jnp.concatenate(rows, axis=0).T

        sides = turned(2)
        for k in range(2):
            scale = inside if k else 1.0
            o_ref[k, r, 0:8, :] = jnp.zeros((8, L), F32)
            o_ref[k, r, TALL - 8 :, :] = jnp.zeros((8, L), F32)
            o_ref[k, r, EDGE : EDGE + L, :] = turned(k) * scale
            o_ref[k, r, EDGE - C : EDGE, :] = sides[W * k : W * k + C] * scale
            o_ref[k, r, EDGE + L : EDGE + L + C, :] = sides[W * k + C : W * k + W] * scale


def main_kernel(
    place_ref, x_ref, above_ref, below_ref, coef_ref, weights_ref, o_ref,
    a_s, b_s, flux_s, slope_s,
):
    first, total = place_ref[1], place_ref[2]
    lane = iota(1, (PART, L))

    for buffer in (a_s, b_s):
        for f in range(F):
            for r in range(DEPTH):
                buffer[f, r, 0:8, :] = jnp.zeros((8, L), F32)
                buffer[f, r, TALL - 8 :, :] = jnp.zeros((8, L), F32)
    for r in range(DEPTH):
        slope_s[r] = -0.25 * inside_of(first, total, r, (PART, L))

    def main_rows(f, row):
        if row < 0:
            return above_ref[pl.ds(8 * f + row + R, S, 8 * F), :]
        if row < 8 * G:
            return x_ref[pl.ds(8 * G * f + row, S, 8 * NALL), :]
        return below_ref[pl.ds(8 * f + row - 8 * G, S, 8 * F), :]

    def side_rows(row):
        if 0 <= row < 8 * G:
            g = row // 8
            value = x_ref[pl.ds(8 * (NMAIN + g // 2) + row % 8, S, 8 * NALL), :]
            return pltpu.roll(value, L - 3 * W, 1) if g % 2 else value
        ref, at = (above_ref, row + R) if row < 0 else (below_ref, row - 8 * G)
        value = ref[pl.ds(8 * S * F + at, S // 2, 8), :]
        return jnp.concatenate([value, pltpu.roll(value, L - 3 * W, 1)], axis=0)

    for r in range(DEPTH):
        for f in range(F):
            rows = [main_rows(f, row_of(b, r)) for b in range(BLOCKS)]
            a_s[f, r, EDGE : EDGE + L, :] = jnp.concatenate(rows, axis=0).T
        rows = [side_rows(row_of(b, r)) for b in range(BLOCKS)]
        sides = jnp.concatenate(rows, axis=0).T
        for f in range(F):
            a_s[f, r, EDGE - C : EDGE, :] = sides[W * f : W * f + C]
            a_s[f, r, EDGE + L : EDGE + L + C, :] = sides[W * f + C : W * f + W]

    parts = [8 + PART * i for i in range((TALL - 16) // PART)]

    def at(ref, r, start, by=0):
        return ref[r, start + by : start + by + PART, :]

    def coef(k, r, start):
        return coef_ref[k, r, start : start + PART, :]

    def neighbours(planes, r, sealed=False):
        up = planes[r - 1] if r else pltpu.roll(planes[-1], S, 1)
        down = planes[r + 1] if r < DEPTH - 1 else pltpu.roll(planes[0], L - S, 1)
        if sealed and r == 0:
            up = jnp.where(lane < S, 0.0, up)
        if sealed and r == DEPTH - 1:
            down = jnp.where(lane >= L - S, 0.0, down)
        return up, down

    def model(src, dst, step):
        h_in, u_in, v_in = src.at[0], src.at[1], src.at[2]
        h_out, u_out, v_out = dst.at[0], dst.at[1], dst.at[2]
        if step == 0:
            for r in range(DEPTH):
                flux_s[r] = coef_ref[0, r] * v_in[r]
        for p in parts:
            flux = [coef(0, r, p) * at(u_in, r, p) for r in range(DEPTH)]
            for r in range(DEPTH):
                up, down = neighbours(flux, r, step == 0)
                out = (down - up) + (at(flux_s, r, p, 1) - at(flux_s, r, p, -1))
                h_out[r, p : p + PART, :] = at(h_in, r, p) + slope_s[r] * out
        for p in parts:
            height = [at(h_out, r, p) for r in range(DEPTH)]
            for r in range(DEPTH):
                up, down = neighbours(height, r)
                u, v = at(u_in, r, p), at(v_in, r, p)
                new_v = v - 0.25 * (at(h_out, r, p, 1) - at(h_out, r, p, -1)) - 0.15 * u
                u_out[r, p : p + PART, :] = u + slope_s[r] * (down - up) + 0.15 * v
                v_out[r, p : p + PART, :] = new_v
                if step < FSTEPS - 1:
                    flux_s[r, p : p + PART, :] = coef(0, r, p) * new_v

    for step in range(FSTEPS):
        model(b_s if step else a_s, b_s, step)

    starts = lax.rem(lane, S) == 0
    for f in range(F):
        for p in parts:
            for r in range(DEPTH):
                ends = pltpu.roll(at(b_s.at[f], r, p), 1, 1)
                a_s[f, r, p : p + PART, :] = at(a_s.at[f], r, p) - jnp.where(starts, 0.0, ends)

    def spread(src, dst):
        for p in parts:
            for f in range(F):
                planes = [at(src.at[f], r, p) for r in range(DEPTH)]
                for r in range(DEPTH):
                    kappa = coef(1, r, p)
                    up, down = neighbours(planes, r)
                    around = (up + down) + (at(src.at[f], r, p, 1) + at(src.at[f], r, p, -1))
                    value = (1.0 - 4.0 * kappa) * planes[r] + kappa * around
                    dst[f, r, p : p + PART, :] = value

    buffers = [a_s, b_s]
    for step in range(DSTEPS):
        spread(buffers[step % 2], buffers[(step + 1) % 2])
    smooth = buffers[DSTEPS % 2]

    weights = weights_ref[...]
    for f in range(F):
        for r in range(DEPTH):
            mixed = lax.dot_general(
                weights,
                smooth[f, r, EDGE : EDGE + L, :],
                (((1,), (1,)), ((), ())),
                precision=lax.Precision.HIGHEST,
                preferred_element_type=F32,
            )
            for b in range(BLOCKS):
                row = row_of(b, r)
                if 0 <= row < 8 * G:
                    o_ref[pl.ds(8 * G * f + row, S, 8 * NMAIN), :] = mixed[S * b : S * b + S]


def unpack_kernel(x_ref, o_ref, sems):
    copies = [
        pltpu.make_async_copy(x_ref.at[c], o_ref.at[:, :, pl.ds(L * c, L)], sems.at[c])
        for c in range(S)
    ]
    for copy in copies:
        copy.start()
    for copy in copies:
        copy.wait()


def kernel(body, out, operands, scalars=0, scratch=(), out_specs=VMEM):
    specs = [SMEM] * scalars + [VMEM] * (len(operands) - scalars)
    return pl.pallas_call(
        body,
        out_shape=out,
        in_specs=specs,
        out_specs=(out_specs,) * len(out) if isinstance(out, tuple) else out_specs,
        scratch_shapes=list(scratch),
        compiler_params=pltpu.CompilerParams(vmem_limit_bytes=12 * 2**20),
    )(*operands)


def kept(x):
    return pltpu.with_memory_space_constraint(x, pltpu.VMEM)


def local(states, terrain, depth_table, spread_table, mixing):
    strips = lax.axis_size("tile")
    rows = states.shape[2]
    chunk = lax.axis_index("sub").astype(jnp.int32)
    first = lax.axis_index("tile").astype(jnp.int32) * rows
    place = jnp.stack([chunk, first, jnp.int32(rows * strips)])
    forth = [(i, i + 1) for i in range(strips - 1)]
    back = [(j, i) for i, j in forth]

    chunks = kernel(pack_kernel, pltpu.VMEM((S, NALL, 8, L), F32), (states[0],))
    held = lax.all_to_all(chunks, "sub", split_axis=0, concat_axis=0, tiled=True)

    edge = pltpu.VMEM((2, 8, L), jnp.int32)
    up, down = kernel(terrain_kernel, (edge, edge), (place, terrain), 1)
    terrain_above = lax.ppermute(down, "tile", forth)
    terrain_below = lax.ppermute(up, "tile", back)
    coef = kernel(
        coef_kernel,
        pltpu.VMEM((2, DEPTH, TALL, L), F32),
        (place, depth_table, spread_table, terrain, kept(terrain_above), kept(terrain_below)),
        3,
        [pltpu.VMEM((3, 8 * (G + 2), L), F32)],
    )
    weights = jnp.kron(jnp.eye(BLOCKS, dtype=F32), mixing)

    halo = pltpu.VMEM((NHALO, 8, L), F32)
    up, down = kernel(
        edge_kernel, (halo, halo), (place, depth_table, kept(held), terrain), 2
    )
    above = lax.ppermute(down, "tile", forth)
    below = lax.ppermute(up, "tile", back)

    plane = (DEPTH, TALL, L)
    mixed = kernel(
        main_kernel,
        pltpu.VMEM((S * NMAIN * 8, L), F32),
        (
            place,
            kept(held.reshape(S * NALL * 8, L)),
            kept(above.reshape(NHALO * 8, L)),
            kept(below.reshape(NHALO * 8, L)),
            kept(coef),
            kept(weights),
        ),
        1,
        [
            pltpu.VMEM((F,) + plane, F32),
            pltpu.VMEM((F,) + plane, F32),
            pltpu.VMEM(plane, F32),
            pltpu.VMEM((DEPTH, PART, L), F32),
        ],
    )
    parts = lax.all_to_all(
        mixed.reshape(S, F, rows, L), "sub", split_axis=0, concat_axis=0, tiled=True
    )
    gradient = kernel(
        unpack_kernel,
        jax.ShapeDtypeStruct((F, rows, S * L), F32),
        (kept(parts),),
        scratch=[pltpu.SemaphoreType.DMA((S,))],
        out_specs=pl.BlockSpec(memory_space=pl.ANY),
    )
    return gradient[None]


def solution(mesh):
    in_specs = (P("sub", None, "tile", None), P("tile", None), P(), P(), P())
    out_specs = P("sub", None, "tile", None)
    return jax.shard_map(local, mesh=mesh, in_specs=in_specs, out_specs=out_specs, check_vma=False)
```

```python
import jax
import jax.numpy as jnp
from jax import lax
from jax.experimental import pallas as pl
from jax.experimental.pallas import tpu as pltpu
from jax.sharding import PartitionSpec as P

FSTEPS = 3
DSTEPS = 3
S = 16
F = 3
G = 4
L = 128
R = 8
C = 9
W = 2 * C
NMAIN = F * G
NALL = NMAIN + 2
NHALO = S * F + S // 2
BLOCKS = 8
DEPTH = 6
EDGE = 16
TALL = L + 2 * EDGE
PART = 16

VMEM = pl.BlockSpec(memory_space=pltpu.VMEM)
SMEM = pl.BlockSpec(memory_space=pltpu.SMEM)
F32 = jnp.float32


def iota(dim, shape=(8, L)):
    return lax.broadcasted_iota(jnp.int32, shape, dim)


def lookup(classes, table):
    value = jnp.full(classes.shape, table[0], F32)
    for i in range(1, table.shape[0]):
        value = jnp.where(classes == i, table[i], value)
    return value


def pack_kernel(x_hbm, o_ref, x_s, sems):
    lane = iota(1)
    copies = [
        [
            pltpu.make_async_copy(
                x_hbm.at[f, pl.ds(8 * g, 8)], x_s.at[f, pl.ds(8 * g, 8)], sems.at[f, g]
            )
            for f in range(F)
        ]
        for g in range(G)
    ]
    for copy in sum(copies, []):
        copy.start()

    def tile(f, g, c):
        return x_s[f, 8 * g : 8 * g + 8, L * (c % S) : L * (c % S) + L]

    for j in range(2):
        for copy in copies[2 * j] + copies[2 * j + 1]:
            copy.wait()
        for c in range(S):
            packed = jnp.zeros((8, L), F32)
            for q in reversed(range(6)):
                f, g = q % 3, 2 * j + q // 3
                o_ref[c, f * G + g] = tile(f, g, c)
                sides = jnp.where(lane < 64, tile(f, g, c + 1), tile(f, g, c - 1))
                sides = pltpu.roll(sides, W * q + C, 1)
                packed = jnp.where(lane < W * q + W, sides, packed)
            o_ref[c, NMAIN + j] = packed


def terrain_tiles(ter_ref, chunk, g):
    def tile(c):
        start = pl.multiple_of(lax.rem(c + S, S) * L, L)
        return ter_ref[8 * g : 8 * g + 8, pl.ds(start, L)]

    return tile(chunk), jnp.where(iota(1) < 64, tile(chunk + 1), tile(chunk - 1))


def edge_kernel(place_ref, depth_ref, x_ref, ter_ref, up_ref, down_ref):
    lane, row = iota(1), iota(0)
    chunk = place_ref[0]

    def send(o_ref, g, inner, edge, turn, sign, halo, flux_at, height_at, low_by, high_by):
        own, sides = terrain_tiles(ter_ref, chunk, inner)
        depth_own = sign * lookup(own, depth_ref)
        depth_sides = pltpu.roll(sign * lookup(sides, depth_ref), W * flux_at + C, 1)
        at_edge = row == edge
        at_height = at_edge & (lane >= W * height_at) & (lane < W * height_at + W)
        by = (W * (height_at - flux_at)) % L
        packed = []
        for t in range(S):
            flux = pltpu.roll(depth_own * x_ref[t, G + inner], turn, 0)
            o_ref[t * F] = x_ref[t, g] + jnp.where(at_edge, flux, 0.0)
            o_ref[t * F + 1] = x_ref[t, G + g]
            o_ref[t * F + 2] = x_ref[t, 2 * G + g]
            columns = x_ref[t, NMAIN + halo]
            flux = pltpu.roll(pltpu.roll(depth_sides * columns, by, 1), turn, 0)
            columns = columns + jnp.where(at_height, flux, 0.0)
            shift = low_by if t < S // 2 else high_by
            packed.append(pltpu.roll(columns, shift, 1) if shift else columns)
        for j in range(S // 2):
            o_ref[S * F + j] = jnp.where(lane < 3 * W, packed[j], packed[j + S // 2])

    send(up_ref, 0, 1, 7, 7, -0.25, 0, 4, 0, 0, 3 * W)
    send(down_ref, 3, 2, 0, 1, 0.25, 1, 1, 3, L - 3 * W, 0)


def terrain_kernel(place_ref, ter_ref, up_ref, down_ref):
    up_ref[0], up_ref[1] = terrain_tiles(ter_ref, place_ref[0], 0)
    down_ref[0], down_ref[1] = terrain_tiles(ter_ref, place_ref[0], G - 1)


def row_of(block, r):
    return DEPTH * block + r - R


def inside_of(first, total, r, shape):
    index = DEPTH * lax.div(iota(1, shape), S) + (r - R) + first
    return ((index >= 0) & (index < total)).astype(F32)


def coef_kernel(place_ref, depth_ref, spread_ref, ter_ref, above_ref, below_ref, o_ref, table_s):
    chunk, first, total = place_ref[0], place_ref[1], place_ref[2]
    lane = iota(1)
    tiles = [(above_ref[0], above_ref[1])]
    tiles += [terrain_tiles(ter_ref, chunk, g) for g in range(G)]
    tiles += [(below_ref[0], below_ref[1])]
    for i, (own, sides) in enumerate(tiles):
        rows = slice(8 * i, 8 * i + 8)
        table_s[0, rows] = lookup(own, depth_ref)
        table_s[1, rows] = lookup(own, spread_ref)
        depth = pltpu.roll(lookup(sides, depth_ref), C, 1)
        spread = pltpu.roll(lookup(sides, spread_ref), W + C, 1)
        table_s[2, rows] = jnp.where(lane < W, depth, spread)
    for r in range(DEPTH):
        inside = inside_of(first, total, r, (1, L))

        def turned(k):
            rows = [
                jnp.broadcast_to(table_s[k, pl.ds(row_of(b, r) + R, 1), :], (S, L))
                for b in range(BLOCKS)
            ]
            return jnp.concatenate(rows, axis=0).T

        sides = turned(2)
        for k in range(2):
            scale = inside if k else 1.0
            o_ref[k, r, 0:8, :] = jnp.zeros((8, L), F32)
            o_ref[k, r, TALL - 8 :, :] = jnp.zeros((8, L), F32)
            o_ref[k, r, EDGE : EDGE + L, :] = turned(k) * scale
            o_ref[k, r, EDGE - C : EDGE, :] = sides[W * k : W * k + C] * scale
            o_ref[k, r, EDGE + L : EDGE + L + C, :] = sides[W * k + C : W * k + W] * scale


def main_kernel(
    place_ref, x_ref, above_ref, below_ref, coef_ref, weights_ref, o_ref,
    a_s, b_s, flux_s, slope_s,
):
    first, total = place_ref[1], place_ref[2]
    lane = iota(1, (PART, L))

    for buffer in (a_s, b_s):
        for f in range(F):
            for r in range(DEPTH):
                buffer[f, r, 0:8, :] = jnp.zeros((8, L), F32)
                buffer[f, r, TALL - 8 :, :] = jnp.zeros((8, L), F32)
    for r in range(DEPTH):
        slope_s[r] = -0.25 * inside_of(first, total, r, (PART, L))

    def main_rows(f, row):
        if row < 0:
            return above_ref[pl.ds(8 * f + row + R, S, 8 * F), :]
        if row < 8 * G:
            return x_ref[pl.ds(8 * G * f + row, S, 8 * NALL), :]
        return below_ref[pl.ds(8 * f + row - 8 * G, S, 8 * F), :]

    def side_rows(row):
        if 0 <= row < 8 * G:
            g = row // 8
            value = x_ref[pl.ds(8 * (NMAIN + g // 2) + row % 8, S, 8 * NALL), :]
            return pltpu.roll(value, L - 3 * W, 1) if g % 2 else value
        ref, at = (above_ref, row + R) if row < 0 else (below_ref, row - 8 * G)
        value = ref[pl.ds(8 * S * F + at, S // 2, 8), :]
        return jnp.concatenate([value, pltpu.roll(value, L - 3 * W, 1)], axis=0)

    for r in range(DEPTH):
        for f in range(F):
            rows = [main_rows(f, row_of(b, r)) for b in range(BLOCKS)]
            a_s[f, r, EDGE : EDGE + L, :] = jnp.concatenate(rows, axis=0).T
        rows = [side_rows(row_of(b, r)) for b in range(BLOCKS)]
        sides = jnp.concatenate(rows, axis=0).T
        for f in range(F):
            a_s[f, r, EDGE - C : EDGE, :] = sides[W * f : W * f + C]
            a_s[f, r, EDGE + L : EDGE + L + C, :] = sides[W * f + C : W * f + W]

    parts = [8 + PART * i for i in range((TALL - 16) // PART)]

    def at(ref, r, start, by=0):
        return ref[r, start + by : start + by + PART, :]

    def coef(k, r, start):
        return coef_ref[k, r, start : start + PART, :]

    def neighbours(planes, r, sealed=False):
        up = planes[r - 1] if r else pltpu.roll(planes[-1], S, 1)
        down = planes[r + 1] if r < DEPTH - 1 else pltpu.roll(planes[0], L - S, 1)
        if sealed and r == 0:
            up = jnp.where(lane < S, 0.0, up)
        if sealed and r == DEPTH - 1:
            down = jnp.where(lane >= L - S, 0.0, down)
        return up, down

    def model(src, dst, step):
        h_in, u_in, v_in = src.at[0], src.at[1], src.at[2]
        h_out, u_out, v_out = dst.at[0], dst.at[1], dst.at[2]
        if step == 0:
            for r in range(DEPTH):
                flux_s[r] = coef_ref[0, r] * v_in[r]
        for p in parts:
            flux = [coef(0, r, p) * at(u_in, r, p) for r in range(DEPTH)]
            for r in range(DEPTH):
                up, down = neighbours(flux, r, step == 0)
                out = (down - up) + (at(flux_s, r, p, 1) - at(flux_s, r, p, -1))
                h_out[r, p : p + PART, :] = at(h_in, r, p) + slope_s[r] * out
        for p in parts:
            height = [at(h_out, r, p) for r in range(DEPTH)]
            for r in range(DEPTH):
                up, down = neighbours(height, r)
                u, v = at(u_in, r, p), at(v_in, r, p)
                new_v = v - 0.25 * (at(h_out, r, p, 1) - at(h_out, r, p, -1)) - 0.15 * u
                u_out[r, p : p + PART, :] = u + slope_s[r] * (down - up) + 0.15 * v
                v_out[r, p : p + PART, :] = new_v
                if step < FSTEPS - 1:
                    flux_s[r, p : p + PART, :] = coef(0, r, p) * new_v

    for step in range(FSTEPS):
        model(b_s if step else a_s, b_s, step)

    starts = lax.rem(lane, S) == 0
    for f in range(F):
        for p in parts:
            for r in range(DEPTH):
                ends = pltpu.roll(at(b_s.at[f], r, p), 1, 1)
                a_s[f, r, p : p + PART, :] = at(a_s.at[f], r, p) - jnp.where(starts, 0.0, ends)

    def spread(src, dst):
        for p in parts:
            for f in range(F):
                planes = [at(src.at[f], r, p) for r in range(DEPTH)]
                for r in range(DEPTH):
                    kappa = coef(1, r, p)
                    up, down = neighbours(planes, r)
                    around = (up + down) + (at(src.at[f], r, p, 1) + at(src.at[f], r, p, -1))
                    value = (1.0 - 4.0 * kappa) * planes[r] + kappa * around
                    dst[f, r, p : p + PART, :] = value

    buffers = [a_s, b_s]
    for step in range(DSTEPS):
        spread(buffers[step % 2], buffers[(step + 1) % 2])
    smooth = buffers[DSTEPS % 2]

    def halves(value):
        high = value.astype(jnp.bfloat16)
        return high, (value - high.astype(F32)).astype(jnp.bfloat16)

    def product(left, right):
        return lax.dot_general(
            left, right, (((1,), (1,)), ((), ())), preferred_element_type=F32
        )

    high, low = halves(weights_ref[...])
    twice = jnp.concatenate([high, high], axis=1)
    for f in range(F):
        for r in range(DEPTH):
            parts = halves(smooth[f, r, EDGE : EDGE + L, :])
            mixed = product(twice, jnp.concatenate(parts, axis=1)) + product(low, parts[0])
            for b in range(BLOCKS):
                row = row_of(b, r)
                if 0 <= row < 8 * G:
                    o_ref[pl.ds(8 * G * f + row, S, 8 * NMAIN), :] = mixed[S * b : S * b + S]


def unpack_kernel(x_ref, o_ref, sems):
    copies = [
        pltpu.make_async_copy(x_ref.at[c], o_ref.at[:, :, pl.ds(L * c, L)], sems.at[c])
        for c in range(S)
    ]
    for copy in copies:
        copy.start()
    for copy in copies:
        copy.wait()


def kernel(body, out, operands, scalars=0, scratch=(), out_specs=VMEM):
    specs = [SMEM] * scalars + [VMEM] * (len(operands) - scalars)
    return pl.pallas_call(
        body,
        out_shape=out,
        in_specs=specs,
        out_specs=(out_specs,) * len(out) if isinstance(out, tuple) else out_specs,
        scratch_shapes=list(scratch),
        compiler_params=pltpu.CompilerParams(vmem_limit_bytes=12 * 2**20),
    )(*operands)


def kept(x):
    return pltpu.with_memory_space_constraint(x, pltpu.VMEM)


def local(states, terrain, depth_table, spread_table, mixing):
    strips = lax.axis_size("tile")
    rows = states.shape[2]
    chunk = lax.axis_index("sub").astype(jnp.int32)
    first = lax.axis_index("tile").astype(jnp.int32) * rows
    place = jnp.stack([chunk, first, jnp.int32(rows * strips)])
    forth = [(i, i + 1) for i in range(strips - 1)]
    back = [(j, i) for i, j in forth]

    chunks = pl.pallas_call(
        pack_kernel,
        out_shape=pltpu.VMEM((S, NALL, 8, L), F32),
        in_specs=[pl.BlockSpec(memory_space=pltpu.HBM)],
        out_specs=VMEM,
        scratch_shapes=[
            pltpu.VMEM((F, rows, S * L), F32),
            pltpu.SemaphoreType.DMA((F, G)),
        ],
        compiler_params=pltpu.CompilerParams(vmem_limit_bytes=12 * 2**20),
    )(pltpu.with_memory_space_constraint(states[0], pltpu.HBM))
    held = lax.all_to_all(chunks, "sub", split_axis=0, concat_axis=0, tiled=True)

    edge = pltpu.VMEM((2, 8, L), jnp.int32)
    up, down = kernel(terrain_kernel, (edge, edge), (place, terrain), 1)
    terrain_above = lax.ppermute(down, "tile", forth)
    terrain_below = lax.ppermute(up, "tile", back)
    coef = kernel(
        coef_kernel,
        pltpu.VMEM((2, DEPTH, TALL, L), F32),
        (place, depth_table, spread_table, terrain, kept(terrain_above), kept(terrain_below)),
        3,
        [pltpu.VMEM((3, 8 * (G + 2), L), F32)],
    )
    weights = jnp.kron(jnp.eye(BLOCKS, dtype=F32), mixing)

    halo = pltpu.VMEM((NHALO, 8, L), F32)
    up, down = kernel(
        edge_kernel, (halo, halo), (place, depth_table, kept(held), terrain), 2
    )
    above = lax.ppermute(down, "tile", forth)
    below = lax.ppermute(up, "tile", back)

    plane = (DEPTH, TALL, L)
    mixed = kernel(
        main_kernel,
        pltpu.VMEM((S * NMAIN * 8, L), F32),
        (
            place,
            kept(held.reshape(S * NALL * 8, L)),
            kept(above.reshape(NHALO * 8, L)),
            kept(below.reshape(NHALO * 8, L)),
            kept(coef),
            kept(weights),
        ),
        1,
        [
            pltpu.VMEM((F,) + plane, F32),
            pltpu.VMEM((F,) + plane, F32),
            pltpu.VMEM(plane, F32),
            pltpu.VMEM((DEPTH, PART, L), F32),
        ],
    )
    parts = lax.all_to_all(
        mixed.reshape(S, F, rows, L), "sub", split_axis=0, concat_axis=0, tiled=True
    )
    gradient = kernel(
        unpack_kernel,
        jax.ShapeDtypeStruct((F, rows, S * L), F32),
        (kept(parts),),
        scratch=[pltpu.SemaphoreType.DMA((S,))],
        out_specs=pl.BlockSpec(memory_space=pl.ANY),
    )
    return gradient[None]


def solution(mesh):
    in_specs = (P("sub", None, "tile", None), P("tile", None), P(), P(), P())
    out_specs = P("sub", None, "tile", None)
    return jax.shard_map(local, mesh=mesh, in_specs=in_specs, out_specs=out_specs, check_vma=False)
```

```python
import jax
import jax.numpy as jnp
from jax import lax
from jax.experimental import pallas as pl
from jax.experimental.pallas import tpu as pltpu
from jax.sharding import PartitionSpec as P

FSTEPS = 3
DSTEPS = 3
S = 16
F = 3
G = 4
L = 128
R = 8
C = 9
W = 2 * C
NOUTER = 2 * F + 1
NINNER = 2 * F + 2
NHALO = S * F + S // 2 + 1
SPARE = 2 * F * W
BLOCKS = 8
DEPTH = 6
EDGE = 16
TALL = L + 2 * EDGE
PART = 16

VMEM = pl.BlockSpec(memory_space=pltpu.VMEM)
SMEM = pl.BlockSpec(memory_space=pltpu.SMEM)
F32 = jnp.float32


def iota(dim, shape=(8, L)):
    return lax.broadcasted_iota(jnp.int32, shape, dim)


def lookup(classes, table):
    value = jnp.full(classes.shape, table[0], F32)
    for i in range(1, table.shape[0]):
        value = jnp.where(classes == i, table[i], value)
    return value


def fetch(pairs, sems):
    copies = [pltpu.make_async_copy(src, dst, sems.at[i]) for i, (src, dst) in enumerate(pairs)]
    for copy in copies:
        copy.start()
    for copy in copies:
        copy.wait()


def pack(o_ref, tile, packed_of):
    lane = iota(1)

    def sides(q, c, at):
        value = jnp.where(lane < 64, tile(q, (c + 1) % S), tile(q, (c - 1) % S))
        return pltpu.roll(value, at + C, 1)

    for c in range(S):
        packed = packed_of(c, sides)
        for q in reversed(range(2 * F)):
            o_ref[c, q] = tile(q, c)
            packed = jnp.where(lane < W * q + W, sides(q, c, W * q), packed)
        o_ref[c, 2 * F] = packed


def outer_kernel(depth_ref, x_hbm, ter_hbm, o_ref, x_s, ter_s, rows_s, sems):
    row = iota(0, (8, S * L))
    groups = [(1, 1), (1, 2), (0, 0), (0, 3), (1, 0), (1, 3), (2, 0), (2, 3)]
    fetch(
        [(ter_hbm.at[pl.ds(8, 16)], ter_s)]
        + [(x_hbm.at[f, pl.ds(8 * g, 8)], x_s.at[f, g]) for f, g in groups],
        sems,
    )

    def flux(g):
        return lookup(ter_s[8 * g - 8 : 8 * g, :], depth_ref) * x_s[1, g]

    rows_s[0] = x_s[0, 0] - jnp.where(row == 7, 0.25 * pltpu.roll(flux(1), 7, 0), 0.0)
    rows_s[1] = x_s[0, 3] + jnp.where(row == 0, 0.25 * pltpu.roll(flux(2), 1, 0), 0.0)

    def tile(q, c):
        cols = slice(L * c, L * c + L)
        if q % F == 0:
            return rows_s[q // F, :, cols]
        return x_s[q % F, q // F * (G - 1), :, cols]

    pack(o_ref, tile, lambda c, sides: jnp.zeros((8, L), F32))


def inner_kernel(x_hbm, o_ref, x_s, rows_s, sems):
    row = iota(0, (8, S * L))
    groups = [(0, 0), (0, 3)] + [(f, g) for f in range(F) for g in (1, 2)]
    fetch([(x_hbm.at[f, pl.ds(8 * g, 8)], x_s.at[f, g]) for f, g in groups], sems)
    rows_s[...] = jnp.where(row == 0, pltpu.roll(x_s[0, 0], 1, 0), pltpu.roll(x_s[0, 3], 1, 0))

    def tile(q, c):
        cols = slice(L * c, L * c + L)
        if q == 2 * F:
            return rows_s[:, cols]
        return x_s[q % F, 1 + q // F, :, cols]

    def packed_of(c, sides):
        o_ref[c, 2 * F + 1] = tile(2 * F, c)
        return sides(2 * F, c, SPARE)

    pack(o_ref, tile, packed_of)


def follow_kernel(x_ref, after_ref, o_ref):
    pass


def terrain_tiles(ter_ref, chunk, g):
    def tile(c):
        start = pl.multiple_of(lax.rem(c + S, S) * L, L)
        return ter_ref[8 * g : 8 * g + 8, pl.ds(start, L)]

    return tile(chunk), jnp.where(iota(1) < 64, tile(chunk + 1), tile(chunk - 1))


def edge_kernel(place_ref, outer_ref, ter_ref, up_ref, down_ref):
    lane = iota(1)

    def send(o_ref, base, g, low_by, high_by):
        own, sides = terrain_tiles(ter_ref, place_ref[0], g)
        o_ref[NHALO - 1] = own.astype(F32)
        sides = pltpu.roll(sides.astype(F32), SPARE + C, 1)
        for t in range(S):
            for f in range(F):
                o_ref[t * F + f] = outer_ref[t, base + f]

        def turned(t, by):
            value = outer_ref[t, 2 * F]
            return pltpu.roll(value, by, 1) if by else value

        for j in range(S // 2):
            columns = jnp.where(
                lane < 3 * W, turned(j, low_by), turned(j + S // 2, high_by)
            )
            o_ref[S * F + j] = jnp.where(lane < SPARE, columns, sides)

    send(up_ref, 0, 0, 0, 3 * W)
    send(down_ref, F, G - 1, L - 3 * W, 0)


def row_of(block, r):
    return DEPTH * block + r - R


def inside_of(first, total, r, shape):
    index = DEPTH * lax.div(iota(1, shape), S) + (r - R) + first
    return ((index >= 0) & (index < total)).astype(F32)


def coef_kernel(place_ref, depth_ref, spread_ref, ter_ref, above_ref, below_ref, o_ref, table_s):
    chunk, first, total = place_ref[0], place_ref[1], place_ref[2]
    lane = iota(1)

    def beside(ref):
        return ref[NHALO - 1], pltpu.roll(ref[S * F], L - SPARE - C, 1)

    tiles = [beside(above_ref)]
    tiles += [terrain_tiles(ter_ref, chunk, g) for g in range(G)]
    tiles += [beside(below_ref)]
    for i, (own, sides) in enumerate(tiles):
        rows = slice(8 * i, 8 * i + 8)
        table_s[0, rows] = lookup(own, depth_ref)
        table_s[1, rows] = lookup(own, spread_ref)
        depth = pltpu.roll(lookup(sides, depth_ref), C, 1)
        spread = pltpu.roll(lookup(sides, spread_ref), W + C, 1)
        table_s[2, rows] = jnp.where(lane < W, depth, spread)
    for r in range(DEPTH):
        inside = inside_of(first, total, r, (1, L))

        def turned(k):
            rows = [
                jnp.broadcast_to(table_s[k, pl.ds(row_of(b, r) + R, 1), :], (S, L))
                for b in range(BLOCKS)
            ]
            return jnp.concatenate(rows, axis=0).T

        sides = turned(2)
        for k in range(2):
            scale = inside if k else 1.0
            o_ref[k, r, 0:8, :] = jnp.zeros((8, L), F32)
            o_ref[k, r, TALL - 8 :, :] = jnp.zeros((8, L), F32)
            o_ref[k, r, EDGE : EDGE + L, :] = turned(k) * scale
            o_ref[k, r, EDGE - C : EDGE, :] = sides[W * k : W * k + C] * scale
            o_ref[k, r, EDGE + L : EDGE + L + C, :] = sides[W * k + C : W * k + W] * scale


def main_kernel(
    place_ref, outer_ref, inner_ref, above_ref, below_ref, coef_ref, weights_ref, o_ref,
    a_s, b_s, flux_s, slope_s,
):
    first, total = place_ref[1], place_ref[2]
    lane = iota(1, (PART, L))

    for buffer in (a_s, b_s):
        for f in range(F):
            for r in range(DEPTH):
                buffer[f, r, 0:8, :] = jnp.zeros((8, L), F32)
                buffer[f, r, TALL - 8 :, :] = jnp.zeros((8, L), F32)
    for r in range(DEPTH):
        slope_s[r] = -0.25 * inside_of(first, total, r, (PART, L))

    def outer_rows(at):
        return outer_ref[pl.ds(at, S, 8 * NOUTER), :]

    def inner_rows(at):
        return inner_ref[pl.ds(at, S, 8 * NINNER), :]

    def main_rows(f, row):
        if row < 0:
            return above_ref[pl.ds(8 * f + row + R, S, 8 * F), :]
        if row >= 8 * G:
            return below_ref[pl.ds(8 * f + row - 8 * G, S, 8 * F), :]
        if f == 0 and row in (7, 24):
            return inner_rows(8 * 7 + row // 8 // 3)
        if 8 <= row < 24:
            return inner_rows(8 * ((row // 8 - 1) * F + f) + row % 8)
        return outer_rows(8 * (row // 24 * F + f) + row % 8)

    def side_rows(row):
        def turned(value, by):
            return pltpu.roll(value, L - by, 1)

        if not 0 <= row < 8 * G:
            ref, at = (above_ref, row + R) if row < 0 else (below_ref, row - 8 * G)
            value = ref[pl.ds(8 * S * F + at, S // 2, 8), :]
            return jnp.concatenate([value, turned(value, 3 * W)], axis=0)
        if 8 <= row < 24:
            value = inner_rows(8 * 6 + row % 8)
            return turned(value, 3 * W) if row >= 16 else value
        value = outer_rows(8 * 6 + row % 8)
        if row >= 24:
            value = turned(value, 3 * W)
        if row in (7, 24):
            height = turned(inner_rows(8 * 6 + row // 8 // 3), SPARE)
            value = jnp.where(lane < W, height, value)
        return value

    for r in range(DEPTH):
        for f in range(F):
            rows = [main_rows(f, row_of(b, r)) for b in range(BLOCKS)]
            a_s[f, r, EDGE : EDGE + L, :] = jnp.concatenate(rows, axis=0).T
        rows = [side_rows(row_of(b, r)) for b in range(BLOCKS)]
        sides = jnp.concatenate(rows, axis=0).T
        for f in range(F):
            a_s[f, r, EDGE - C : EDGE, :] = sides[W * f : W * f + C]
            a_s[f, r, EDGE + L : EDGE + L + C, :] = sides[W * f + C : W * f + W]

    parts = [8 + PART * i for i in range((TALL - 16) // PART)]

    def at(ref, r, start, by=0):
        return ref[r, start + by : start + by + PART, :]

    def coef(k, r, start):
        return coef_ref[k, r, start : start + PART, :]

    def neighbours(planes, r, sealed=False):
        up = planes[r - 1] if r else pltpu.roll(planes[-1], S, 1)
        down = planes[r + 1] if r < DEPTH - 1 else pltpu.roll(planes[0], L - S, 1)
        if sealed and r == 0:
            up = jnp.where(lane < S, 0.0, up)
        if sealed and r == DEPTH - 1:
            down = jnp.where(lane >= L - S, 0.0, down)
        return up, down

    def model(src, dst, step):
        h_in, u_in, v_in = src.at[0], src.at[1], src.at[2]
        h_out, u_out, v_out = dst.at[0], dst.at[1], dst.at[2]
        if step == 0:
            for r in range(DEPTH):
                flux_s[r] = coef_ref[0, r] * v_in[r]
        for p in parts:
            flux = [coef(0, r, p) * at(u_in, r, p) for r in range(DEPTH)]
            for r in range(DEPTH):
                up, down = neighbours(flux, r, step == 0)
                out = (down - up) + (at(flux_s, r, p, 1) - at(flux_s, r, p, -1))
                h_out[r, p : p + PART, :] = at(h_in, r, p) + slope_s[r] * out
        for p in parts:
            height = [at(h_out, r, p) for r in range(DEPTH)]
            for r in range(DEPTH):
                up, down = neighbours(height, r)
                u, v = at(u_in, r, p), at(v_in, r, p)
                new_v = v - 0.25 * (at(h_out, r, p, 1) - at(h_out, r, p, -1)) - 0.15 * u
                u_out[r, p : p + PART, :] = u + slope_s[r] * (down - up) + 0.15 * v
                v_out[r, p : p + PART, :] = new_v
                if step < FSTEPS - 1:
                    flux_s[r, p : p + PART, :] = coef(0, r, p) * new_v

    for step in range(FSTEPS):
        model(b_s if step else a_s, b_s, step)

    starts = lax.rem(lane, S) == 0
    for f in range(F):
        for p in parts:
            for r in range(DEPTH):
                ends = pltpu.roll(at(b_s.at[f], r, p), 1, 1)
                a_s[f, r, p : p + PART, :] = at(a_s.at[f], r, p) - jnp.where(starts, 0.0, ends)

    def spread(src, dst):
        for p in parts:
            for f in range(F):
                planes = [at(src.at[f], r, p) for r in range(DEPTH)]
                for r in range(DEPTH):
                    kappa = coef(1, r, p)
                    up, down = neighbours(planes, r)
                    around = (up + down) + (at(src.at[f], r, p, 1) + at(src.at[f], r, p, -1))
                    value = (1.0 - 4.0 * kappa) * planes[r] + kappa * around
                    dst[f, r, p : p + PART, :] = value

    buffers = [a_s, b_s]
    for step in range(DSTEPS):
        spread(buffers[step % 2], buffers[(step + 1) % 2])
    smooth = buffers[DSTEPS % 2]

    def halves(value):
        high = value.astype(jnp.bfloat16)
        return high, (value - high.astype(F32)).astype(jnp.bfloat16)

    def product(left, right):
        return lax.dot_general(
            left, right, (((1,), (1,)), ((), ())), preferred_element_type=F32
        )

    high, low = halves(weights_ref[...])
    twice = jnp.concatenate([high, high], axis=1)
    for f in range(F):
        for r in range(DEPTH):
            parts = halves(smooth[f, r, EDGE : EDGE + L, :])
            mixed = product(twice, jnp.concatenate(parts, axis=1)) + product(low, parts[0])
            for b in range(BLOCKS):
                row = row_of(b, r)
                if 0 <= row < 8 * G:
                    o_ref[pl.ds(8 * G * f + row, S, 8 * G * F), :] = mixed[S * b : S * b + S]


def unpack_kernel(x_ref, o_ref, sems):
    copies = [
        pltpu.make_async_copy(x_ref.at[c], o_ref.at[:, :, pl.ds(L * c, L)], sems.at[c])
        for c in range(S)
    ]
    for copy in copies:
        copy.start()
    for copy in copies:
        copy.wait()


def kernel(body, out, operands, scalars=0, scratch=(), out_specs=VMEM, cost=None):
    specs = [SMEM] * scalars + [VMEM] * (len(operands) - scalars)
    return pl.pallas_call(
        body,
        out_shape=out,
        in_specs=specs,
        out_specs=(out_specs,) * len(out) if isinstance(out, tuple) else out_specs,
        scratch_shapes=list(scratch),
        cost_estimate=cost,
        compiler_params=pltpu.CompilerParams(vmem_limit_bytes=12 * 2**20),
    )(*operands)


def kept(x):
    return pltpu.with_memory_space_constraint(x, pltpu.VMEM)


def far(x):
    return pltpu.with_memory_space_constraint(x, pltpu.HBM)


def local(states, terrain, depth_table, spread_table, mixing):
    strips = lax.axis_size("tile")
    rows = states.shape[2]
    chunk = lax.axis_index("sub").astype(jnp.int32)
    first = lax.axis_index("tile").astype(jnp.int32) * rows
    place = jnp.stack([chunk, first, jnp.int32(rows * strips)])
    forth = [(i, i + 1) for i in range(strips - 1)]
    back = [(j, i) for i, j in forth]

    def to_chunks(value):
        return lax.all_to_all(value, "sub", split_axis=0, concat_axis=0, tiled=True)

    hbm = pl.BlockSpec(memory_space=pltpu.HBM)
    limit = pltpu.CompilerParams(vmem_limit_bytes=12 * 2**20)
    outer = pl.pallas_call(
        outer_kernel,
        out_shape=pltpu.VMEM((S, NOUTER, 8, L), F32),
        in_specs=[SMEM, hbm, hbm],
        out_specs=VMEM,
        scratch_shapes=[
            pltpu.VMEM((F, G, 8, S * L), F32),
            pltpu.VMEM((16, S * L), jnp.int32),
            pltpu.VMEM((2, 8, S * L), F32),
            pltpu.SemaphoreType.DMA((9,)),
        ],
        compiler_params=limit,
    )(far(depth_table), far(states[0]), far(terrain))
    outer = to_chunks(outer)
    halo = pltpu.VMEM((NHALO, 8, L), F32)
    up, down = kernel(edge_kernel, (halo, halo), (place, kept(outer), terrain), 1)
    above = lax.ppermute(down, "tile", forth)
    below = lax.ppermute(up, "tile", back)
    inner = pl.pallas_call(
        inner_kernel,
        out_shape=pltpu.VMEM((S, NINNER, 8, L), F32),
        in_specs=[hbm],
        out_specs=VMEM,
        scratch_shapes=[
            pltpu.VMEM((F, G, 8, S * L), F32),
            pltpu.VMEM((8, S * L), F32),
            pltpu.SemaphoreType.DMA((8,)),
        ],
        compiler_params=limit,
    )(far(states[0]))
    anywhere = pl.BlockSpec(memory_space=pl.ANY)
    inner = pl.pallas_call(
        follow_kernel,
        out_shape=jax.ShapeDtypeStruct(inner.shape, F32),
        in_specs=[anywhere, anywhere],
        out_specs=anywhere,
        input_output_aliases={0: 0},
    )(inner, up)
    inner = to_chunks(inner)
    coef = kernel(
        coef_kernel,
        pltpu.VMEM((2, DEPTH, TALL, L), F32),
        (place, depth_table, spread_table, terrain, kept(above), kept(below)),
        3,
        [pltpu.VMEM((3, 8 * (G + 2), L), F32)],
        cost=pl.CostEstimate(flops=10**11, bytes_accessed=10**6, transcendentals=0),
    )
    weights = jnp.kron(jnp.eye(BLOCKS, dtype=F32), mixing)

    plane = (DEPTH, TALL, L)
    mixed = kernel(
        main_kernel,
        pltpu.VMEM((S * F * rows, L), F32),
        (
            place,
            kept(outer.reshape(S * NOUTER * 8, L)),
            kept(inner.reshape(S * NINNER * 8, L)),
            kept(above.reshape(NHALO * 8, L)),
            kept(below.reshape(NHALO * 8, L)),
            kept(coef),
            kept(weights),
        ),
        1,
        [
            pltpu.VMEM((F,) + plane, F32),
            pltpu.VMEM((F,) + plane, F32),
            pltpu.VMEM(plane, F32),
            pltpu.VMEM((DEPTH, PART, L), F32),
        ],
    )
    parts = lax.all_to_all(
        mixed.reshape(S, F, rows, L), "sub", split_axis=0, concat_axis=0, tiled=True
    )
    gradient = kernel(
        unpack_kernel,
        jax.ShapeDtypeStruct((F, rows, S * L), F32),
        (kept(parts),),
        scratch=[pltpu.SemaphoreType.DMA((S,))],
        out_specs=pl.BlockSpec(memory_space=pl.ANY),
    )
    return gradient[None]


def solution(mesh):
    in_specs = (P("sub", None, "tile", None), P("tile", None), P(), P(), P())
    out_specs = P("sub", None, "tile", None)
    return jax.shard_map(local, mesh=mesh, in_specs=in_specs, out_specs=out_specs, check_vma=False)
```

```python
import jax
import jax.numpy as jnp
from jax import lax
from jax.experimental import pallas as pl
from jax.experimental.pallas import tpu as pltpu
from jax.sharding import PartitionSpec as P

FSTEPS = 3
DSTEPS = 3
S = 16
F = 3
G = 4
L = 128
R = 8
C = 9
W = 2 * C
NPART = 2 * F + 1
NHALO = S * F + S // 2 + 1
SPARE = 2 * F * W
BLOCKS = 8
DEPTH = 6
EDGE = 16
TALL = L + 2 * EDGE
PART = 16

VMEM = pl.BlockSpec(memory_space=pltpu.VMEM)
SMEM = pl.BlockSpec(memory_space=pltpu.SMEM)
F32 = jnp.float32


def iota(dim, shape=(8, L)):
    return lax.broadcasted_iota(jnp.int32, shape, dim)


def lookup(classes, table):
    value = jnp.full(classes.shape, table[0], F32)
    for i in range(1, table.shape[0]):
        value = jnp.where(classes == i, table[i], value)
    return value


def fetch(pairs, sems):
    copies = [pltpu.make_async_copy(src, dst, sems.at[i]) for i, (src, dst) in enumerate(pairs)]
    for copy in copies:
        copy.start()
    for copy in copies:
        copy.wait()


def pack(o_ref, tile):
    lane = iota(1)

    def sides(q, c, at):
        value = jnp.where(lane < 64, tile(q, (c + 1) % S), tile(q, (c - 1) % S))
        return pltpu.roll(value, at + C, 1)

    for c in range(S):
        packed = jnp.zeros((8, L), F32)
        for q in reversed(range(2 * F)):
            o_ref[c, q] = tile(q, c)
            packed = jnp.where(lane < W * q + W, sides(q, c, W * q), packed)
        o_ref[c, 2 * F] = packed


def outer_kernel(depth_ref, x_hbm, ter_hbm, o_ref, x_s, ter_s, rows_s, sems):
    row = iota(0, (8, S * L))
    groups = [(1, 1), (1, 2), (0, 0), (0, 3), (1, 0), (1, 3), (2, 0), (2, 3)]
    fetch(
        [(ter_hbm.at[pl.ds(8, 16)], ter_s)]
        + [(x_hbm.at[f, pl.ds(8 * g, 8)], x_s.at[f, g]) for f, g in groups],
        sems,
    )

    def flux(g):
        return lookup(ter_s[8 * g - 8 : 8 * g, :], depth_ref) * x_s[1, g]

    rows_s[0] = x_s[0, 0] - jnp.where(row == 7, 0.25 * pltpu.roll(flux(1), 7, 0), 0.0)
    rows_s[1] = x_s[0, 3] + jnp.where(row == 0, 0.25 * pltpu.roll(flux(2), 1, 0), 0.0)

    def tile(q, c):
        cols = slice(L * c, L * c + L)
        if q % F == 0:
            return rows_s[q // F, :, cols]
        return x_s[q % F, q // F * (G - 1), :, cols]

    pack(o_ref, tile)


def inner_kernel(x_hbm, o_ref, x_s, sems):
    groups = [(f, g) for f in range(F) for g in range(2)]
    fetch([(x_hbm.at[f, pl.ds(8 * g + 8, 8)], x_s.at[f, g]) for f, g in groups], sems)

    def tile(q, c):
        return x_s[q % F, q // F, :, L * c : L * c + L]

    pack(o_ref, tile)


def follow_kernel(x_ref, after_ref, o_ref):
    pass


def terrain_tiles(ter_ref, chunk, g):
    def tile(c):
        start = pl.multiple_of(lax.rem(c + S, S) * L, L)
        return ter_ref[8 * g : 8 * g + 8, pl.ds(start, L)]

    return tile(chunk), jnp.where(iota(1) < 64, tile(chunk + 1), tile(chunk - 1))


def edge_kernel(place_ref, outer_ref, ter_ref, up_ref, down_ref):
    lane = iota(1)

    def send(o_ref, base, g, low_by, high_by):
        own, sides = terrain_tiles(ter_ref, place_ref[0], g)
        o_ref[NHALO - 1] = own.astype(F32)
        sides = pltpu.roll(sides.astype(F32), SPARE + C, 1)
        for t in range(S):
            for f in range(F):
                o_ref[t * F + f] = outer_ref[t, base + f]

        def turned(t, by):
            value = outer_ref[t, 2 * F]
            return pltpu.roll(value, by, 1) if by else value

        for j in range(S // 2):
            columns = jnp.where(
                lane < 3 * W, turned(j, low_by), turned(j + S // 2, high_by)
            )
            o_ref[S * F + j] = jnp.where(lane < SPARE, columns, sides)

    send(up_ref, 0, 0, 0, 3 * W)
    send(down_ref, F, G - 1, L - 3 * W, 0)


def row_of(block, r):
    return DEPTH * block + r - R


def inside_of(first, total, r, shape):
    index = DEPTH * lax.div(iota(1, shape), S) + (r - R) + first
    return ((index >= 0) & (index < total)).astype(F32)


def coef_kernel(place_ref, depth_ref, spread_ref, ter_ref, above_ref, below_ref, o_ref, table_s):
    chunk, first, total = place_ref[0], place_ref[1], place_ref[2]
    lane = iota(1)

    def beside(ref):
        return ref[NHALO - 1], pltpu.roll(ref[S * F], L - SPARE - C, 1)

    tiles = [beside(above_ref)]
    tiles += [terrain_tiles(ter_ref, chunk, g) for g in range(G)]
    tiles += [beside(below_ref)]
    for i, (own, sides) in enumerate(tiles):
        rows = slice(8 * i, 8 * i + 8)
        table_s[0, rows] = lookup(own, depth_ref)
        table_s[1, rows] = lookup(own, spread_ref)
        depth = pltpu.roll(lookup(sides, depth_ref), C, 1)
        spread = pltpu.roll(lookup(sides, spread_ref), W + C, 1)
        table_s[2, rows] = jnp.where(lane < W, depth, spread)
    for r in range(DEPTH):
        inside = inside_of(first, total, r, (1, L))

        def turned(k):
            rows = [
                jnp.broadcast_to(table_s[k, pl.ds(row_of(b, r) + R, 1), :], (S, L))
                for b in range(BLOCKS)
            ]
            return jnp.concatenate(rows, axis=0).T

        sides = turned(2)
        for k in range(2):
            scale = inside if k else 1.0
            o_ref[k, r, 0:8, :] = jnp.zeros((8, L), F32)
            o_ref[k, r, TALL - 8 :, :] = jnp.zeros((8, L), F32)
            o_ref[k, r, EDGE : EDGE + L, :] = turned(k) * scale
            o_ref[k, r, EDGE - C : EDGE, :] = sides[W * k : W * k + C] * scale
            o_ref[k, r, EDGE + L : EDGE + L + C, :] = sides[W * k + C : W * k + W] * scale


def main_kernel(
    place_ref, outer_ref, inner_ref, above_ref, below_ref, coef_ref, weights_ref, o_ref,
    a_s, b_s, flux_s, slope_s,
):
    first, total = place_ref[1], place_ref[2]
    lane = iota(1, (PART, L))

    for buffer in (a_s, b_s):
        for f in range(F):
            for r in range(DEPTH):
                buffer[f, r, 0:8, :] = jnp.zeros((8, L), F32)
                buffer[f, r, TALL - 8 :, :] = jnp.zeros((8, L), F32)
    for r in range(DEPTH):
        slope_s[r] = -0.25 * inside_of(first, total, r, (PART, L))

    def outer_rows(at):
        return outer_ref[pl.ds(at, S, 8 * NPART), :]

    def inner_rows(at):
        return inner_ref[pl.ds(at, S, 8 * NPART), :]

    def main_rows(f, row):
        if row < 0:
            return above_ref[pl.ds(8 * f + row + R, S, 8 * F), :]
        if row >= 8 * G:
            return below_ref[pl.ds(8 * f + row - 8 * G, S, 8 * F), :]
        if 8 <= row < 24:
            return inner_rows(8 * ((row // 8 - 1) * F + f) + row % 8)
        return outer_rows(8 * (row // 24 * F + f) + row % 8)

    def side_rows(row):
        def turned(value, by):
            return pltpu.roll(value, L - by, 1)

        if not 0 <= row < 8 * G:
            ref, at = (above_ref, row + R) if row < 0 else (below_ref, row - 8 * G)
            value = ref[pl.ds(8 * S * F + at, S // 2, 8), :]
            return jnp.concatenate([value, turned(value, 3 * W)], axis=0)
        if 8 <= row < 24:
            value = inner_rows(8 * 6 + row % 8)
            return turned(value, 3 * W) if row >= 16 else value
        value = outer_rows(8 * 6 + row % 8)
        return turned(value, 3 * W) if row >= 24 else value

    for r in range(DEPTH):
        for f in range(F):
            rows = [main_rows(f, row_of(b, r)) for b in range(BLOCKS)]
            a_s[f, r, EDGE : EDGE + L, :] = jnp.concatenate(rows, axis=0).T
        rows = [side_rows(row_of(b, r)) for b in range(BLOCKS)]
        sides = jnp.concatenate(rows, axis=0).T
        for f in range(F):
            a_s[f, r, EDGE - C : EDGE, :] = sides[W * f : W * f + C]
            a_s[f, r, EDGE + L : EDGE + L + C, :] = sides[W * f + C : W * f + W]

    block = lax.div(iota(1, (TALL, L)), S)
    for row, beyond, sign in ((7, 8, 0.25), (24, 23, -0.25)):
        (at_block, r), flux_r = divmod(row + R, DEPTH), (beyond + R) % DEPTH
        flux = sign * coef_ref[0, flux_r] * a_s[1, flux_r]
        a_s[0, r] = a_s[0, r] + jnp.where(block == at_block, flux, 0.0)

    parts = [8 + PART * i for i in range((TALL - 16) // PART)]

    def at(ref, r, start, by=0):
        return ref[r, start + by : start + by + PART, :]

    def coef(k, r, start):
        return coef_ref[k, r, start : start + PART, :]

    def neighbours(planes, r, sealed=False):
        up = planes[r - 1] if r else pltpu.roll(planes[-1], S, 1)
        down = planes[r + 1] if r < DEPTH - 1 else pltpu.roll(planes[0], L - S, 1)
        if sealed and r == 0:
            up = jnp.where(lane < S, 0.0, up)
        if sealed and r == DEPTH - 1:
            down = jnp.where(lane >= L - S, 0.0, down)
        return up, down

    def model(src, dst, step):
        h_in, u_in, v_in = src.at[0], src.at[1], src.at[2]
        h_out, u_out, v_out = dst.at[0], dst.at[1], dst.at[2]
        if step == 0:
            for r in range(DEPTH):
                flux_s[r] = coef_ref[0, r] * v_in[r]
        for p in parts:
            flux = [coef(0, r, p) * at(u_in, r, p) for r in range(DEPTH)]
            for r in range(DEPTH):
                up, down = neighbours(flux, r, step == 0)
                out = (down - up) + (at(flux_s, r, p, 1) - at(flux_s, r, p, -1))
                h_out[r, p : p + PART, :] = at(h_in, r, p) + slope_s[r] * out
        for p in parts:
            height = [at(h_out, r, p) for r in range(DEPTH)]
            for r in range(DEPTH):
                up, down = neighbours(height, r)
                u, v = at(u_in, r, p), at(v_in, r, p)
                new_v = v - 0.25 * (at(h_out, r, p, 1) - at(h_out, r, p, -1)) - 0.15 * u
                u_out[r, p : p + PART, :] = u + slope_s[r] * (down - up) + 0.15 * v
                v_out[r, p : p + PART, :] = new_v
                if step < FSTEPS - 1:
                    flux_s[r, p : p + PART, :] = coef(0, r, p) * new_v

    for step in range(FSTEPS):
        model(b_s if step else a_s, b_s, step)

    starts = lax.rem(lane, S) == 0
    for f in range(F):
        for p in parts:
            for r in range(DEPTH):
                ends = pltpu.roll(at(b_s.at[f], r, p), 1, 1)
                a_s[f, r, p : p + PART, :] = at(a_s.at[f], r, p) - jnp.where(starts, 0.0, ends)

    def spread(src, dst):
        for p in parts:
            for f in range(F):
                planes = [at(src.at[f], r, p) for r in range(DEPTH)]
                for r in range(DEPTH):
                    kappa = coef(1, r, p)
                    up, down = neighbours(planes, r)
                    around = (up + down) + (at(src.at[f], r, p, 1) + at(src.at[f], r, p, -1))
                    value = (1.0 - 4.0 * kappa) * planes[r] + kappa * around
                    dst[f, r, p : p + PART, :] = value

    buffers = [a_s, b_s]
    for step in range(DSTEPS):
        spread(buffers[step % 2], buffers[(step + 1) % 2])
    smooth = buffers[DSTEPS % 2]

    def halves(value):
        high = value.astype(jnp.bfloat16)
        return high, (value - high.astype(F32)).astype(jnp.bfloat16)

    def product(left, right):
        return lax.dot_general(
            left, right, (((1,), (1,)), ((), ())), preferred_element_type=F32
        )

    high, low = halves(weights_ref[...])
    twice = jnp.concatenate([high, high], axis=1)
    for f in range(F):
        for r in range(DEPTH):
            parts = halves(smooth[f, r, EDGE : EDGE + L, :])
            mixed = product(twice, jnp.concatenate(parts, axis=1)) + product(low, parts[0])
            for b in range(BLOCKS):
                row = row_of(b, r)
                if 0 <= row < 8 * G:
                    o_ref[pl.ds(8 * G * f + row, S, 8 * G * F), :] = mixed[S * b : S * b + S]


def unpack_kernel(x_ref, o_ref, sems):
    copies = [
        pltpu.make_async_copy(x_ref.at[c], o_ref.at[:, :, pl.ds(L * c, L)], sems.at[c])
        for c in range(S)
    ]
    for copy in copies:
        copy.start()
    for copy in copies:
        copy.wait()


def kernel(body, out, operands, scalars=0, scratch=(), out_specs=VMEM, cost=None):
    specs = [SMEM] * scalars + [VMEM] * (len(operands) - scalars)
    return pl.pallas_call(
        body,
        out_shape=out,
        in_specs=specs,
        out_specs=(out_specs,) * len(out) if isinstance(out, tuple) else out_specs,
        scratch_shapes=list(scratch),
        cost_estimate=cost,
        compiler_params=pltpu.CompilerParams(vmem_limit_bytes=12 * 2**20),
    )(*operands)


def kept(x):
    return pltpu.with_memory_space_constraint(x, pltpu.VMEM)


def far(x):
    return pltpu.with_memory_space_constraint(x, pltpu.HBM)


def local(states, terrain, depth_table, spread_table, mixing):
    strips = lax.axis_size("tile")
    rows = states.shape[2]
    chunk = lax.axis_index("sub").astype(jnp.int32)
    first = lax.axis_index("tile").astype(jnp.int32) * rows
    place = jnp.stack([chunk, first, jnp.int32(rows * strips)])
    forth = [(i, i + 1) for i in range(strips - 1)]
    back = [(j, i) for i, j in forth]

    def to_chunks(value):
        return lax.all_to_all(value, "sub", split_axis=0, concat_axis=0, tiled=True)

    hbm = pl.BlockSpec(memory_space=pltpu.HBM)
    limit = pltpu.CompilerParams(vmem_limit_bytes=12 * 2**20)
    outer = pl.pallas_call(
        outer_kernel,
        out_shape=pltpu.VMEM((S, NPART, 8, L), F32),
        in_specs=[SMEM, hbm, hbm],
        out_specs=VMEM,
        scratch_shapes=[
            pltpu.VMEM((F, G, 8, S * L), F32),
            pltpu.VMEM((16, S * L), jnp.int32),
            pltpu.VMEM((2, 8, S * L), F32),
            pltpu.SemaphoreType.DMA((9,)),
        ],
        compiler_params=limit,
    )(far(depth_table), far(states[0]), far(terrain))
    outer = to_chunks(outer)
    halo = pltpu.VMEM((NHALO, 8, L), F32)
    up, down = kernel(edge_kernel, (halo, halo), (place, kept(outer), terrain), 1)
    above = lax.ppermute(down, "tile", forth)
    below = lax.ppermute(up, "tile", back)
    inner = pl.pallas_call(
        inner_kernel,
        out_shape=pltpu.VMEM((S, NPART, 8, L), F32),
        in_specs=[hbm],
        out_specs=VMEM,
        scratch_shapes=[
            pltpu.VMEM((F, 2, 8, S * L), F32),
            pltpu.SemaphoreType.DMA((2 * F,)),
        ],
        compiler_params=limit,
    )(far(states[0]))
    anywhere = pl.BlockSpec(memory_space=pl.ANY)
    inner = pl.pallas_call(
        follow_kernel,
        out_shape=jax.ShapeDtypeStruct(inner.shape, F32),
        in_specs=[anywhere, anywhere],
        out_specs=anywhere,
        input_output_aliases={0: 0},
    )(inner, up)
    inner = to_chunks(inner)
    coef = kernel(
        coef_kernel,
        pltpu.VMEM((2, DEPTH, TALL, L), F32),
        (place, depth_table, spread_table, terrain, kept(above), kept(below)),
        3,
        [pltpu.VMEM((3, 8 * (G + 2), L), F32)],
        cost=pl.CostEstimate(flops=10**11, bytes_accessed=10**6, transcendentals=0),
    )
    weights = jnp.kron(jnp.eye(BLOCKS, dtype=F32), mixing)

    plane = (DEPTH, TALL, L)
    mixed = kernel(
        main_kernel,
        pltpu.VMEM((S * F * rows, L), F32),
        (
            place,
            kept(outer.reshape(S * NPART * 8, L)),
            kept(inner.reshape(S * NPART * 8, L)),
            kept(above.reshape(NHALO * 8, L)),
            kept(below.reshape(NHALO * 8, L)),
            kept(coef),
            kept(weights),
        ),
        1,
        [
            pltpu.VMEM((F,) + plane, F32),
            pltpu.VMEM((F,) + plane, F32),
            pltpu.VMEM(plane, F32),
            pltpu.VMEM((DEPTH, PART, L), F32),
        ],
    )
    parts = lax.all_to_all(
        mixed.reshape(S, F, rows, L), "sub", split_axis=0, concat_axis=0, tiled=True
    )
    gradient = kernel(
        unpack_kernel,
        jax.ShapeDtypeStruct((F, rows, S * L), F32),
        (kept(parts),),
        scratch=[pltpu.SemaphoreType.DMA((S,))],
        out_specs=pl.BlockSpec(memory_space=pl.ANY),
    )
    return gradient[None]


def solution(mesh):
    in_specs = (P("sub", None, "tile", None), P("tile", None), P(), P(), P())
    out_specs = P("sub", None, "tile", None)
    return jax.shard_map(local, mesh=mesh, in_specs=in_specs, out_specs=out_specs, check_vma=False)
```

```python
import jax
import jax.numpy as jnp
from jax import lax
from jax.experimental import pallas as pl
from jax.experimental.pallas import tpu as pltpu
from jax.sharding import PartitionSpec as P

FSTEPS = 3
DSTEPS = 3
S = 16
F = 3
G = 4
L = 128
R = 8
C = 9
W = 2 * C
NPART = 2 * F + 1
NHALO = S * F + S // 2 + 1
SPARE = 2 * F * W
BLOCKS = 8
DEPTH = 6
EDGE = 16
TALL = L + 2 * EDGE
PART = 16

VMEM = pl.BlockSpec(memory_space=pltpu.VMEM)
SMEM = pl.BlockSpec(memory_space=pltpu.SMEM)
F32 = jnp.float32


def iota(dim, shape=(8, L)):
    return lax.broadcasted_iota(jnp.int32, shape, dim)


def lookup(classes, table):
    value = jnp.full(classes.shape, table[0], F32)
    for i in range(1, table.shape[0]):
        value = jnp.where(classes == i, table[i], value)
    return value


def fetch(pairs, sems):
    copies = [pltpu.make_async_copy(src, dst, sems.at[i]) for i, (src, dst) in enumerate(pairs)]
    for copy in copies:
        copy.start()
    return copies


def arrive(copies):
    for copy in copies:
        copy.wait()


def pack(o_ref, tile):
    lane = iota(1)

    def sides(q, c, at):
        value = jnp.where(lane < 64, tile(q, (c + 1) % S), tile(q, (c - 1) % S))
        return pltpu.roll(value, at + C, 1)

    for c in range(S):
        packed = jnp.zeros((8, L), F32)
        for q in reversed(range(2 * F)):
            o_ref[c, q] = tile(q, c)
            packed = jnp.where(lane < W * q + W, sides(q, c, W * q), packed)
        o_ref[c, 2 * F] = packed


def outer_kernel(depth_ref, x_hbm, ter_hbm, o_ref, x_s, ter_s, rows_s, sems):
    row = iota(0, (8, S * L))
    groups = [(1, 1), (1, 2), (0, 0), (0, 3), (1, 0), (1, 3), (2, 0), (2, 3)]
    copies = fetch(
        [(ter_hbm.at[pl.ds(8, 16)], ter_s)]
        + [(x_hbm.at[f, pl.ds(8 * g, 8)], x_s.at[f, g]) for f, g in groups],
        sems,
    )

    arrive(copies[:5])

    def flux(g):
        return lookup(ter_s[8 * g - 8 : 8 * g, :], depth_ref) * x_s[1, g]

    rows_s[0] = x_s[0, 0] - jnp.where(row == 7, 0.25 * pltpu.roll(flux(1), 7, 0), 0.0)
    rows_s[1] = x_s[0, 3] + jnp.where(row == 0, 0.25 * pltpu.roll(flux(2), 1, 0), 0.0)

    arrive(copies[5:])

    def tile(q, c):
        cols = slice(L * c, L * c + L)
        if q % F == 0:
            return rows_s[q // F, :, cols]
        return x_s[q % F, q // F * (G - 1), :, cols]

    pack(o_ref, tile)


def inner_kernel(x_hbm, o_ref, x_s, sems):
    groups = [(f, g) for f in range(F) for g in range(2)]
    arrive(fetch([(x_hbm.at[f, pl.ds(8 * g + 8, 8)], x_s.at[f, g]) for f, g in groups], sems))

    def tile(q, c):
        return x_s[q % F, q // F, :, L * c : L * c + L]

    pack(o_ref, tile)


def follow_kernel(x_ref, after_ref, o_ref):
    pass


def terrain_tiles(ter_ref, chunk, g):
    def tile(c):
        start = pl.multiple_of(lax.rem(c + S, S) * L, L)
        return ter_ref[8 * g : 8 * g + 8, pl.ds(start, L)]

    return tile(chunk), jnp.where(iota(1) < 64, tile(chunk + 1), tile(chunk - 1))


def edge_kernel(place_ref, outer_ref, ter_ref, up_ref, down_ref):
    lane = iota(1)

    def send(o_ref, base, g, low_by, high_by):
        own, sides = terrain_tiles(ter_ref, place_ref[0], g)
        o_ref[NHALO - 1] = own.astype(F32)
        sides = pltpu.roll(sides.astype(F32), SPARE + C, 1)
        for t in range(S):
            for f in range(F):
                o_ref[t * F + f] = outer_ref[t, base + f]

        def turned(t, by):
            value = outer_ref[t, 2 * F]
            return pltpu.roll(value, by, 1) if by else value

        for j in range(S // 2):
            columns = jnp.where(
                lane < 3 * W, turned(j, low_by), turned(j + S // 2, high_by)
            )
            o_ref[S * F + j] = jnp.where(lane < SPARE, columns, sides)

    send(up_ref, 0, 0, 0, 3 * W)
    send(down_ref, F, G - 1, L - 3 * W, 0)


def row_of(block, r):
    return DEPTH * block + r - R


def inside_of(first, total, r, shape):
    index = DEPTH * lax.div(iota(1, shape), S) + (r - R) + first
    return ((index >= 0) & (index < total)).astype(F32)


def coef_kernel(place_ref, depth_ref, spread_ref, ter_ref, above_ref, below_ref, o_ref, table_s):
    chunk, first, total = place_ref[0], place_ref[1], place_ref[2]
    lane = iota(1)

    def beside(ref):
        return ref[NHALO - 1], pltpu.roll(ref[S * F], L - SPARE - C, 1)

    tiles = [beside(above_ref)]
    tiles += [terrain_tiles(ter_ref, chunk, g) for g in range(G)]
    tiles += [beside(below_ref)]
    for i, (own, sides) in enumerate(tiles):
        rows = slice(8 * i, 8 * i + 8)
        table_s[0, rows] = lookup(own, depth_ref)
        table_s[1, rows] = lookup(own, spread_ref)
        depth = pltpu.roll(lookup(sides, depth_ref), C, 1)
        spread = pltpu.roll(lookup(sides, spread_ref), W + C, 1)
        table_s[2, rows] = jnp.where(lane < W, depth, spread)
    for r in range(DEPTH):
        inside = inside_of(first, total, r, (1, L))

        def turned(k):
            rows = [
                jnp.broadcast_to(table_s[k, pl.ds(row_of(b, r) + R, 1), :], (S, L))
                for b in range(BLOCKS)
            ]
            return jnp.concatenate(rows, axis=0).T

        sides = turned(2)
        for k in range(2):
            scale = inside if k else 1.0
            o_ref[k, r, 0:8, :] = jnp.zeros((8, L), F32)
            o_ref[k, r, TALL - 8 :, :] = jnp.zeros((8, L), F32)
            o_ref[k, r, EDGE : EDGE + L, :] = turned(k) * scale
            o_ref[k, r, EDGE - C : EDGE, :] = sides[W * k : W * k + C] * scale
            o_ref[k, r, EDGE + L : EDGE + L + C, :] = sides[W * k + C : W * k + W] * scale


def main_kernel(
    place_ref, outer_ref, inner_ref, above_ref, below_ref, coef_ref, weights_ref, o_ref,
    a_s, b_s, flux_s, slope_s,
):
    first, total = place_ref[1], place_ref[2]
    lane = iota(1, (PART, L))

    for buffer in (a_s, b_s):
        for f in range(F):
            for r in range(DEPTH):
                buffer[f, r, 0:8, :] = jnp.zeros((8, L), F32)
                buffer[f, r, TALL - 8 :, :] = jnp.zeros((8, L), F32)
    for r in range(DEPTH):
        slope_s[r] = -0.25 * inside_of(first, total, r, (PART, L))

    def outer_rows(at):
        return outer_ref[pl.ds(at, S, 8 * NPART), :]

    def inner_rows(at):
        return inner_ref[pl.ds(at, S, 8 * NPART), :]

    def main_rows(f, row):
        if row < 0:
            return above_ref[pl.ds(8 * f + row + R, S, 8 * F), :]
        if row >= 8 * G:
            return below_ref[pl.ds(8 * f + row - 8 * G, S, 8 * F), :]
        if 8 <= row < 24:
            return inner_rows(8 * ((row // 8 - 1) * F + f) + row % 8)
        return outer_rows(8 * (row // 24 * F + f) + row % 8)

    def side_rows(row):
        def turned(value, by):
            return pltpu.roll(value, L - by, 1)

        if not 0 <= row < 8 * G:
            ref, at = (above_ref, row + R) if row < 0 else (below_ref, row - 8 * G)
            value = ref[pl.ds(8 * S * F + at, S // 2, 8), :]
            return jnp.concatenate([value, turned(value, 3 * W)], axis=0)
        if 8 <= row < 24:
            value = inner_rows(8 * 6 + row % 8)
            return turned(value, 3 * W) if row >= 16 else value
        value = outer_rows(8 * 6 + row % 8)
        return turned(value, 3 * W) if row >= 24 else value

    for r in range(DEPTH):
        for f in range(F):
            rows = [main_rows(f, row_of(b, r)) for b in range(BLOCKS)]
            a_s[f, r, EDGE : EDGE + L, :] = jnp.concatenate(rows, axis=0).T
        rows = [side_rows(row_of(b, r)) for b in range(BLOCKS)]
        sides = jnp.concatenate(rows, axis=0).T
        for f in range(F):
            a_s[f, r, EDGE - C : EDGE, :] = sides[W * f : W * f + C]
            a_s[f, r, EDGE + L : EDGE + L + C, :] = sides[W * f + C : W * f + W]

    block = lax.div(iota(1, (TALL, L)), S)
    for row, beyond, sign in ((7, 8, 0.25), (24, 23, -0.25)):
        (at_block, r), flux_r = divmod(row + R, DEPTH), (beyond + R) % DEPTH
        flux = sign * coef_ref[0, flux_r] * a_s[1, flux_r]
        a_s[0, r] = a_s[0, r] + jnp.where(block == at_block, flux, 0.0)

    parts = [8 + PART * i for i in range((TALL - 16) // PART)]

    def at(ref, r, start, by=0):
        return ref[r, start + by : start + by + PART, :]

    def coef(k, r, start):
        return coef_ref[k, r, start : start + PART, :]

    def neighbours(planes, r, sealed=False):
        up = planes[r - 1] if r else pltpu.roll(planes[-1], S, 1)
        down = planes[r + 1] if r < DEPTH - 1 else pltpu.roll(planes[0], L - S, 1)
        if sealed and r == 0:
            up = jnp.where(lane < S, 0.0, up)
        if sealed and r == DEPTH - 1:
            down = jnp.where(lane >= L - S, 0.0, down)
        return up, down

    def model(src, dst, step):
        h_in, u_in, v_in = src.at[0], src.at[1], src.at[2]
        h_out, u_out, v_out = dst.at[0], dst.at[1], dst.at[2]
        if step == 0:
            for r in range(DEPTH):
                flux_s[r] = coef_ref[0, r] * v_in[r]
        for p in parts:
            flux = [coef(0, r, p) * at(u_in, r, p) for r in range(DEPTH)]
            for r in range(DEPTH):
                up, down = neighbours(flux, r, step == 0)
                out = (down - up) + (at(flux_s, r, p, 1) - at(flux_s, r, p, -1))
                h_out[r, p : p + PART, :] = at(h_in, r, p) + slope_s[r] * out
        for p in parts:
            height = [at(h_out, r, p) for r in range(DEPTH)]
            for r in range(DEPTH):
                up, down = neighbours(height, r)
                u, v = at(u_in, r, p), at(v_in, r, p)
                new_v = v - 0.25 * (at(h_out, r, p, 1) - at(h_out, r, p, -1)) - 0.15 * u
                u_out[r, p : p + PART, :] = u + slope_s[r] * (down - up) + 0.15 * v
                v_out[r, p : p + PART, :] = new_v
                if step < FSTEPS - 1:
                    flux_s[r, p : p + PART, :] = coef(0, r, p) * new_v

    for step in range(FSTEPS):
        model(b_s if step else a_s, b_s, step)

    starts = lax.rem(lane, S) == 0
    for f in range(F):
        for p in parts:
            for r in range(DEPTH):
                ends = pltpu.roll(at(b_s.at[f], r, p), 1, 1)
                a_s[f, r, p : p + PART, :] = at(a_s.at[f], r, p) - jnp.where(starts, 0.0, ends)

    def spread(src, dst):
        for p in parts:
            for f in range(F):
                planes = [at(src.at[f], r, p) for r in range(DEPTH)]
                for r in range(DEPTH):
                    kappa = coef(1, r, p)
                    up, down = neighbours(planes, r)
                    around = (up + down) + (at(src.at[f], r, p, 1) + at(src.at[f], r, p, -1))
                    value = (1.0 - 4.0 * kappa) * planes[r] + kappa * around
                    dst[f, r, p : p + PART, :] = value

    buffers = [a_s, b_s]
    for step in range(DSTEPS):
        spread(buffers[step % 2], buffers[(step + 1) % 2])
    smooth = buffers[DSTEPS % 2]

    def halves(value):
        high = value.astype(jnp.bfloat16)
        return high, (value - high.astype(F32)).astype(jnp.bfloat16)

    def product(left, right):
        return lax.dot_general(
            left, right, (((1,), (1,)), ((), ())), preferred_element_type=F32
        )

    high, low = halves(weights_ref[...])
    twice = jnp.concatenate([high, high], axis=1)
    for f in range(F):
        for r in range(DEPTH):
            parts = halves(smooth[f, r, EDGE : EDGE + L, :])
            mixed = product(twice, jnp.concatenate(parts, axis=1)) + product(low, parts[0])
            for b in range(BLOCKS):
                row = row_of(b, r)
                if 0 <= row < 8 * G:
                    o_ref[pl.ds(8 * G * f + row, S, 8 * G * F), :] = mixed[S * b : S * b + S]


def unpack_kernel(x_ref, o_ref, sems):
    copies = [
        pltpu.make_async_copy(x_ref.at[c, f], o_ref.at[f, :, pl.ds(L * c, L)], sems.at[c, f])
        for f in range(F)
        for c in range(S)
    ]
    for copy in copies:
        copy.start()
    for copy in copies:
        copy.wait()


def kernel(body, out, operands, scalars=0, scratch=(), out_specs=VMEM, cost=None):
    specs = [SMEM] * scalars + [VMEM] * (len(operands) - scalars)
    return pl.pallas_call(
        body,
        out_shape=out,
        in_specs=specs,
        out_specs=(out_specs,) * len(out) if isinstance(out, tuple) else out_specs,
        scratch_shapes=list(scratch),
        cost_estimate=cost,
        compiler_params=pltpu.CompilerParams(vmem_limit_bytes=12 * 2**20),
    )(*operands)


def kept(x):
    return pltpu.with_memory_space_constraint(x, pltpu.VMEM)


def far(x):
    return pltpu.with_memory_space_constraint(x, pltpu.HBM)


def local(states, terrain, depth_table, spread_table, mixing):
    strips = lax.axis_size("tile")
    rows = states.shape[2]
    chunk = lax.axis_index("sub").astype(jnp.int32)
    first = lax.axis_index("tile").astype(jnp.int32) * rows
    place = jnp.stack([chunk, first, jnp.int32(rows * strips)])
    forth = [(i, i + 1) for i in range(strips - 1)]
    back = [(j, i) for i, j in forth]

    def to_chunks(value):
        return lax.all_to_all(value, "sub", split_axis=0, concat_axis=0, tiled=True)

    hbm = pl.BlockSpec(memory_space=pltpu.HBM)
    limit = pltpu.CompilerParams(vmem_limit_bytes=12 * 2**20)
    outer = pl.pallas_call(
        outer_kernel,
        out_shape=pltpu.VMEM((S, NPART, 8, L), F32),
        in_specs=[SMEM, hbm, hbm],
        out_specs=VMEM,
        scratch_shapes=[
            pltpu.VMEM((F, G, 8, S * L), F32),
            pltpu.VMEM((16, S * L), jnp.int32),
            pltpu.VMEM((2, 8, S * L), F32),
            pltpu.SemaphoreType.DMA((9,)),
        ],
        compiler_params=limit,
    )(far(depth_table), far(states[0]), far(terrain))
    outer = to_chunks(outer)
    halo = pltpu.VMEM((NHALO, 8, L), F32)
    up, down = kernel(edge_kernel, (halo, halo), (place, kept(outer), terrain), 1)
    above = lax.ppermute(down, "tile", forth)
    below = lax.ppermute(up, "tile", back)
    inner = pl.pallas_call(
        inner_kernel,
        out_shape=pltpu.VMEM((S, NPART, 8, L), F32),
        in_specs=[hbm],
        out_specs=VMEM,
        scratch_shapes=[
            pltpu.VMEM((F, 2, 8, S * L), F32),
            pltpu.SemaphoreType.DMA((2 * F,)),
        ],
        compiler_params=limit,
    )(far(states[0]))
    anywhere = pl.BlockSpec(memory_space=pl.ANY)
    inner = pl.pallas_call(
        follow_kernel,
        out_shape=jax.ShapeDtypeStruct(inner.shape, F32),
        in_specs=[anywhere, anywhere],
        out_specs=anywhere,
        input_output_aliases={0: 0},
    )(inner, up)
    inner = to_chunks(inner)
    coef = kernel(
        coef_kernel,
        pltpu.VMEM((2, DEPTH, TALL, L), F32),
        (place, depth_table, spread_table, terrain, kept(above), kept(below)),
        3,
        [pltpu.VMEM((3, 8 * (G + 2), L), F32)],
        cost=pl.CostEstimate(flops=10**11, bytes_accessed=10**6, transcendentals=0),
    )
    weights = jnp.kron(jnp.eye(BLOCKS, dtype=F32), mixing)

    plane = (DEPTH, TALL, L)
    mixed = kernel(
        main_kernel,
        pltpu.VMEM((S * F * rows, L), F32),
        (
            place,
            kept(outer.reshape(S * NPART * 8, L)),
            kept(inner.reshape(S * NPART * 8, L)),
            kept(above.reshape(NHALO * 8, L)),
            kept(below.reshape(NHALO * 8, L)),
            kept(coef),
            kept(weights),
        ),
        1,
        [
            pltpu.VMEM((F,) + plane, F32),
            pltpu.VMEM((F,) + plane, F32),
            pltpu.VMEM(plane, F32),
            pltpu.VMEM((DEPTH, PART, L), F32),
        ],
    )
    parts = lax.all_to_all(
        mixed.reshape(S, F, rows, L), "sub", split_axis=0, concat_axis=0, tiled=True
    )
    gradient = kernel(
        unpack_kernel,
        jax.ShapeDtypeStruct((F, rows, S * L), F32),
        (kept(parts),),
        scratch=[pltpu.SemaphoreType.DMA((S, F))],
        out_specs=pl.BlockSpec(memory_space=pl.ANY),
    )
    return gradient[None]


def solution(mesh):
    in_specs = (P("sub", None, "tile", None), P("tile", None), P(), P(), P())
    out_specs = P("sub", None, "tile", None)
    return jax.shard_map(local, mesh=mesh, in_specs=in_specs, out_specs=out_specs, check_vma=False)
```
